32 devices in a mesh: wide: 8 (over z, y), narrow: 4 (over x, core).
Axes of the slice: x: 2, y: 2, z: 4, core: 2. Of those that a mesh axis runs over, the one named last changes fastest.
Arguments:
- features: bfloat16 [768, 65536], P('narrow', 'wide'), may hold values from -6 to 6
- owner_of: int32 [4096, 16, 1], P('wide'), may hold values from 0 to 7; in each aligned block of 8192 rows (0 to 8191, 8192 to 16383, ..., all dimensions but the last counted through in order) at most 1536 rows name the same one
- row_of: int32 [4096, 16], P('wide'), may hold values from 0 to 8191
- w_self: bfloat16 [768, 256], P('narrow'), may hold values from -0.15625 to 0.15625
- w_neighbor: bfloat16 [768, 256], P('narrow'), may hold values from -0.15625 to 0.15625
- cotangent: bfloat16 [4096, 256], P(('wide', 'narrow')), may hold values from -0.09375 to 0.09375
Outputs:
- hidden: bfloat16 [4096, 256], P(('wide', 'narrow'))
- grad_self: float32 [768, 256], P('narrow')
- grad_neighbor: float32 [768, 256], P('narrow')
The draws below stay inside these ranges and needn't reach their ends.
Inputs may be any that keep to these rules, and one draw needn't show every extreme that they name: `owner_of`: among the 8192 rows read by the targets of one index of wide, no owner is named more than 1536 times, and in every draw some owner is named exactly 1536 times by some index.
All inputs are finite; a program needn't handle non-finite values.
Results may differ from the reference program's by a relative error of at most 0.0054.
Values may be sent and summed in bfloat16 or wider, within the bound.
No kernel may reach another device: no remote copies, remote signals or barrier semaphores. Data moves between devices by JAX's collectives and lax.ppermute only.
A program may use at most 64 MiB of HBM per device.

```python
import math
import jax
import jax.numpy as jnp
import numpy as np
from jax import lax

F = 768
H = 256
NODE_DEV = 8192
TGT_DEV = 512
FANOUT = 15
REQ = 16
CAP = 1536
NODES = 65536
TARGETS = 4096
N_WIDE = 8


def plant(result, rng, low, top_value):
    place = [jax.random.randint(jax.random.fold_in(rng, axis), (), 0, length) for axis, length in enumerate(result.shape)]
    widest = result.shape.index(max(result.shape))
    next_to = place[:widest] + [(place[widest] + 1) % result.shape[widest]] + place[widest + 1:]
    return result.at[tuple(place)].set(low).at[tuple(next_to)].set(top_value)


def block_scale(stream_key, extent, pieces, low, largest):
    def one(position, shards_of):
        steps = jax.random.uniform(jax.random.fold_in(jax.random.fold_in(stream_key, 6), position), (shards_of,), jnp.float32, low / len(pieces), largest / len(pieces))
        return jnp.repeat(jnp.exp(steps), extent[position] // shards_of).reshape((-1,) + (1,) * (len(extent) - position - 1))

    gain = one(*pieces[0])
    for cut in pieces[1:]:
        gain = gain * one(*cut)
    return gain


def shared_out(stream_key, own, number, rows, count, top, limit, lean):
    sequence = jax.random.permutation(stream_key, count)
    heavy_load, ordinary = shares(count, rows * top, limit, lean, True), shares(count, rows * top, limit, lean, False)
    places = jnp.arange(count)

    def named(tallies, turn):
        used = int((tallies > 0).sum())
        fixed = max(1, used // 4)
        passed = fixed + (places - fixed + turn * (used - fixed)) % max(1, count - fixed)
        return jnp.zeros((count,), jnp.int32).at[sequence[jnp.where(places < fixed, places, passed)]].set(jnp.asarray(tallies, jnp.int32))

    tallies = jnp.where(number % 4 == 0, named(heavy_load, number // 4), named(ordinary, number - number // 4 - 1))
    mixed = jax.random.permutation(jax.random.fold_in(own, 3), count)
    source_of, sink = mixed[0:count // 2 * 2:2], mixed[1:count // 2 * 2:2]
    slack = jnp.minimum(tallies[source_of] - 1, limit - tallies[sink]) // 2
    slack = jnp.where((source_of == sequence[0]) | (sink == sequence[0]) | (tallies[sink] == 0), 0, jnp.maximum(slack, 0))
    passed = jax.random.randint(jax.random.fold_in(own, 4), (count // 2,), 0, 1 << 20) % (slack + 1)
    tallies = tallies.at[source_of].add(-passed).at[sink].add(passed)
    members = jnp.searchsorted(jnp.cumsum(tallies), jnp.arange(rows * top), side="right").astype(jnp.int32)
    listing = members.reshape(top, rows).T
    listing = listing[jax.random.permutation(jax.random.fold_in(own, 1), rows)]
    turn = jax.random.randint(jax.random.fold_in(own, 2), (rows, 1), 0, top)
    return jnp.take_along_axis(listing, (jnp.arange(top)[None, :] + turn) % top, axis=1)


def shares(number_of, total, limit, skew, full):
    portions = [(1 << 20) // math.isqrt(rank ** skew) + 1 for rank in range(1, number_of + 1)]
    largest = limit if full else min(limit, max(-(-total // number_of), total * portions[0] // sum(portions)))
    least = 1 if total - largest >= number_of - 1 else 0
    counts, rest = [largest] + [least] * (number_of - 1), total - largest - least * (number_of - 1)
    while rest > 0:
        candidates = [i for i in range(1, number_of) if counts[i] < largest] or [i for i in range(1, number_of) if counts[i] < limit]
        mass, remaining = sum([portions[i] for i in candidates]), rest
        for i in candidates:
            extra = min(limit - counts[i], max(1, remaining * portions[i] // mass), rest)
            counts[i] = counts[i] + extra
            rest = rest - extra
    return np.array(counts)


def bell_draw(own_key, dims, scale, limit, shards=(), kind=jnp.bfloat16):
    entries = scale * jax.random.normal(own_key, dims, jnp.float32)
    if shards:
        entries = entries * block_scale(own_key, dims, shards, -0.22, 0.18)
    return jnp.clip(entries, -limit, limit).astype(kind)


def setup_inputs(seed: int = 0) -> dict:
    streams_of = jax.random.split(jax.random.key(seed), 7)
    features = bell_draw(streams_of[0], (F, NODES), 1.0, 6.0, ((0, 4), (1, 8)))
    owner_of_keys = jax.random.split(jax.random.fold_in(streams_of[1], 1), TARGETS * REQ // (TGT_DEV * REQ))
    owner_of_turns = jax.random.permutation(jax.random.fold_in(streams_of[1], 3), TARGETS * REQ // (TGT_DEV * REQ))
    owner_of = jax.vmap(lambda own, number: shared_out(jax.random.fold_in(streams_of[1], 2), own, number, TGT_DEV * REQ, N_WIDE, 1, CAP, 2))(owner_of_keys, owner_of_turns).reshape((TARGETS, REQ, 1))
    row_of = plant(jax.random.randint(streams_of[2], (TARGETS, REQ), 0, NODE_DEV), jax.random.fold_in(streams_of[2], 1), 0, NODE_DEV - 1).astype(jnp.int32)
    w_self = bell_draw(streams_of[3], (F, H), (2 * F) ** -0.5, 0.15625, ((0, 4),))
    w_neighbor = bell_draw(streams_of[4], (F, H), (2 * F) ** -0.5, 0.15625, ((0, 4),))
    cotangent = bell_draw(streams_of[5], (TARGETS, H), (1.0 / TARGETS ** 0.5), 0.09375, ((0, 32),))
    return dict(features=features, owner_of=owner_of, row_of=row_of, w_self=w_self, w_neighbor=w_neighbor, cotangent=cotangent)


def activation(value):
    return jax.nn.gelu(value, approximate=True)

def reference(features, owner_of, row_of, w_self, w_neighbor, cotangent):
    blocks = TARGETS // TGT_DEV
    owner_blocks = owner_of[:, :, 0].reshape(blocks, TGT_DEV, REQ)
    row_blocks = row_of.reshape(blocks, TGT_DEV, REQ)
    cot_blocks = cotangent.reshape(blocks, TGT_DEV, H)

    def step(carry, inputs):
        grad_s, grad_n = carry
        owners, rows, cots = inputs
        node = (owners * NODE_DEV + rows).astype(jnp.int32)
        gathered = jnp.transpose(jnp.take(features, node, axis=1), (1, 2, 0))
        self_rows = gathered[:, 0]
        pooled = (lax.optimization_barrier(jnp.sum(gathered[:, 1:].astype(jnp.float32), axis=1)) / FANOUT).astype(jnp.bfloat16)
        preact = jnp.dot(self_rows, w_self, preferred_element_type=jnp.float32) + jnp.dot(pooled, w_neighbor, preferred_element_type=jnp.float32)
        value, pullback = jax.vjp(activation, preact)
        slope = pullback(cots.astype(jnp.float32))[0].astype(jnp.bfloat16)
        grad_s = grad_s + jnp.dot(self_rows.T, slope, preferred_element_type=jnp.float32)
        grad_n = grad_n + jnp.dot(pooled.T, slope, preferred_element_type=jnp.float32)
        return ((grad_s, grad_n), value.astype(jnp.bfloat16))
    start = (jnp.zeros((F, H), jnp.float32), jnp.zeros((F, H), jnp.float32))
    (grad_self, grad_neighbor), hidden = lax.scan(step, start, (owner_blocks, row_blocks, cot_blocks))
    return (hidden.reshape(TARGETS, H), grad_self, grad_neighbor)
```

```python
import functools

import jax
import jax.numpy as jnp
from jax import lax
from jax.experimental import pallas as pl
from jax.experimental.pallas import tpu as pltpu
from jax.sharding import PartitionSpec as P

FANOUT = 15
BF16 = jnp.bfloat16
F32 = jnp.float32
VMEM_BYTES = 56 * 1024 * 1024


def activation(value):
    return jax.nn.gelu(value, approximate=True)


def contract_rows(left, right):
    return lax.dot_general(
        left, right, (((0,), (0,)), ((), ())), preferred_element_type=F32
    )


def list_kernel(wide_count, capacity, row_bits, tgt_bits, owner_ref, row_ref, out_ref):
    requests, targets = owner_ref.shape
    hi_count = out_ref.shape[0]
    owners = owner_ref[...]
    masks = jnp.concatenate(
        [jnp.where(owners == w, 1.0, 0.0).astype(BF16) for w in range(wide_count)], axis=0
    )
    lanes = lax.broadcasted_iota(jnp.int32, (targets, targets), 1)
    upper = jnp.where(lax.broadcasted_iota(jnp.int32, (targets, targets), 0) < lanes, 1.0, 0.0)
    within = jnp.dot(masks, upper.astype(BF16), preferred_element_type=F32)
    total = wide_count * requests
    first = lax.broadcasted_iota(jnp.int32, (total, total), 0)
    second = lax.broadcasted_iota(jnp.int32, (total, total), 1)
    lower = jnp.where((second < first) & (second >= first - first % requests), 1.0, 0.0)
    before = jnp.dot(lower.astype(BF16), masks, preferred_element_type=F32)
    offset = jnp.sum(before, axis=1, keepdims=True)
    ranked = masks.astype(F32) * (within + offset)
    slot = jnp.zeros(owners.shape, F32)
    for w in range(wide_count):
        slot = slot + ranked[w * requests : (w + 1) * requests]
    position = owners * capacity + slot.astype(jnp.int32)
    high = position >> 7
    low = position & 127
    target = lax.broadcasted_iota(jnp.int32, owners.shape, 1)
    kind = jnp.where(lax.broadcasted_iota(jnp.int32, owners.shape, 0) == 0, 0, 1)
    code = row_ref[...] | ((target | ((kind | 2) << tgt_bits)) << row_bits)
    parts = [(code & 255).astype(F32), ((code >> 8) & 255).astype(F32), (code >> 16).astype(F32)]
    high_iota = lax.broadcasted_iota(jnp.int32, (hi_count, targets), 0)
    low_iota = lax.broadcasted_iota(jnp.int32, (128, targets), 0)
    sums = jnp.zeros((hi_count, 384), F32)
    for j in range(requests):
        left = jnp.where(high_iota == high[j : j + 1], 1.0, 0.0).astype(BF16)
        hit = low_iota == low[j : j + 1]
        right = jnp.concatenate(
            [jnp.where(hit, part[j : j + 1], 0.0).astype(BF16) for part in parts], axis=0
        )
        sums = sums + lax.dot_general(
            left, right, (((1,), (1,)), ((), ())), preferred_element_type=F32
        )
    out_ref[...] = (sums[:, :128] + sums[:, 128:256] * 256.0 + sums[:, 256:] * 65536.0).astype(
        jnp.int32
    )


def table_kernel(feature_ref, out_ref):
    block = feature_ref[...].astype(F32)
    rest = block[128:]
    out_ref[0] = jnp.transpose(block[:128])
    out_ref[1] = jnp.transpose(jnp.concatenate([rest, rest], axis=0))


def owner_kernel(unroll, rows_ref, place_ref, key_ref, table_ref, weight_ref,
                 keep_ref, send_ref, sums_ref, held, dense):
    source = pl.program_id(0)
    capacity = held.shape[1]
    targets = 128
    quarters = 4
    table = table_ref.reshape(2, table_ref.shape[1], 1, 128)
    base = source * capacity

    def fetch(step, carry):
        for u in range(unroll):
            i = step * unroll + u
            r = rows_ref[base + i]
            held[0, i] = table[0, r]
            held[1, i] = table[1, r]
        return carry

    lax.fori_loop(0, capacity // unroll, fetch, 0)
    flat = held.reshape(2, capacity, 128)
    dense[:, :128] = flat[0].astype(BF16)
    dense[:, 128:] = flat[1].astype(BF16)
    lane = lax.broadcasted_iota(jnp.int32, (targets, 128), 1)
    narrow = place_ref[0]

    def quarter(q, carry):
        row = lax.broadcasted_iota(jnp.int32, (2 * targets, capacity), 0)
        wanted = jnp.where(row < targets, row, row + (quarters - 1) * targets) + q * targets
        onehot = jnp.where(wanted == key_ref[0], 1.0, 0.0).astype(BF16)
        both = jnp.dot(onehot, dense[...], preferred_element_type=F32)
        own = both[:targets]
        mean = both[targets:] / FANOUT
        mid = jnp.where(lane < 64, own[:, 128:], mean[:, 128:])
        summed = jnp.concatenate([own[:, :128], mid, mean[:, :128]], axis=1).astype(BF16)
        preact = jnp.dot(summed, weight_ref[...], preferred_element_type=F32).astype(BF16)
        other = q ^ narrow
        core = other & 1
        chip = other >> 1
        sums_ref[2 * core + chip, 0] = summed

        @pl.when(core == 0)
        def _():
            keep_ref[chip, 0] = preact

        @pl.when(core == 1)
        def _():
            send_ref[chip, 0] = preact

        return carry

    lax.fori_loop(0, quarters, quarter, 0)


def swap(value, axis, bit):
    count = lax.axis_size(axis)
    return lax.ppermute(value, axis, [(i, i ^ bit) for i in range(count)])


def on_device(features, owner_of, row_of, w_self, w_neighbor, cotangent):
    wide_count = lax.axis_size("wide")
    targets, requests = row_of.shape
    columns, nodes = features.shape
    hidden_units = w_self.shape[1]
    total = targets * requests
    capacity = max(2, 3 * total // (2 * wide_count))
    row_bits = (nodes - 1).bit_length()
    tgt_bits = (targets - 1).bit_length()
    share = targets // 4

    lists = pl.pallas_call(
        functools.partial(list_kernel, wide_count, capacity, row_bits, tgt_bits),
        out_shape=jax.ShapeDtypeStruct((wide_count * capacity // 128, 128), jnp.int32),
        compiler_params=pltpu.CompilerParams(vmem_limit_bytes=VMEM_BYTES),
        name="lists",
    )(jnp.transpose(owner_of.reshape(targets, requests)), jnp.transpose(row_of))
    asked = lax.all_to_all(
        lists.reshape(wide_count, capacity), "wide", split_axis=0, concat_axis=0, tiled=True
    )

    block = 1024
    table = pl.pallas_call(
        table_kernel,
        grid=(nodes // block,),
        in_specs=[pl.BlockSpec((columns, block), lambda i: (0, i))],
        out_specs=pl.BlockSpec((2, block, 128), lambda i: (0, i, 0)),
        out_shape=jax.ShapeDtypeStruct((2, nodes, 128), F32),
        cost_estimate=pl.CostEstimate(flops=0, bytes_accessed=24 * 1024 * 1024, transcendentals=0),
        name="table",
    )(features)

    rows = (asked & (nodes - 1)).reshape(wide_count * capacity)
    tail = asked >> row_bits
    keys = jnp.where(tail >= 2 * targets, tail - 2 * targets, -1).reshape(wide_count, 1, capacity)
    weights = jnp.concatenate(
        [w_self[:128], w_self[128:], w_neighbor[128:], w_neighbor[:128]], axis=0
    )
    unroll = next(u for u in (64, 32, 16, 8, 4, 2, 1) if capacity % u == 0)
    place = lax.axis_index("narrow").astype(jnp.int32).reshape(1)
    halves = jax.ShapeDtypeStruct((2, wide_count, share, hidden_units), BF16)
    keep, send, sums = pl.pallas_call(
        functools.partial(owner_kernel, unroll),
        grid_spec=pltpu.PrefetchScalarGridSpec(
            num_scalar_prefetch=2,
            grid=(wide_count,),
            in_specs=[
                pl.BlockSpec((1, 1, capacity), lambda s, *_: (s, 0, 0)),
                pl.BlockSpec((2, nodes, 128), lambda s, *_: (0, 0, 0)),
                pl.BlockSpec((2 * columns, hidden_units), lambda s, *_: (0, 0)),
            ],
            out_specs=[
                pl.BlockSpec((2, 1, share, hidden_units), lambda s, *_: (0, s, 0, 0)),
                pl.BlockSpec((2, 1, share, hidden_units), lambda s, *_: (0, s, 0, 0)),
                pl.BlockSpec((4, 1, share, 2 * columns), lambda s, *_: (0, s, 0, 0)),
            ],
            scratch_shapes=[
                pltpu.VMEM((2, capacity, 1, 128), F32),
                pltpu.VMEM((capacity, 256), BF16),
            ],
        ),
        out_shape=[
            halves,
            halves,
            jax.ShapeDtypeStruct((4, wide_count, share, 2 * columns), BF16),
        ],
        compiler_params=pltpu.CompilerParams(vmem_limit_bytes=VMEM_BYTES),
        name="owner",
    )(rows, place, keys, table, weights)

    paired = keep.astype(F32) + swap(send, "narrow", 1).astype(F32)
    quartet = paired[0] + swap(paired[1].astype(BF16), "narrow", 2).astype(F32)
    pieces = lax.all_to_all(
        quartet.astype(BF16), "wide", split_axis=0, concat_axis=0, tiled=True
    )
    preact = jnp.sum(pieces.astype(F32), axis=0)
    value, pullback = jax.vjp(activation, preact)
    hidden = value.astype(BF16)
    slope = pullback(cotangent.astype(F32))[0].astype(BF16)

    slopes = lax.all_to_all(
        jnp.broadcast_to(slope[None], (wide_count, share, hidden_units)),
        "wide", split_axis=0, concat_axis=0, tiled=True,
    )
    across = swap(slopes, "narrow", 2)
    both = jnp.stack([slopes, across])
    beside = swap(both, "narrow", 1)
    rows_per = wide_count * share
    grads = contract_rows(
        sums[:2].reshape(2 * rows_per, 2 * columns), both.reshape(2 * rows_per, hidden_units)
    ) + contract_rows(
        sums[2:].reshape(2 * rows_per, 2 * columns), beside.reshape(2 * rows_per, hidden_units)
    )
    slices = grads.astype(BF16).reshape(wide_count, 2 * columns // wide_count, hidden_units)
    own = jnp.sum(
        lax.all_to_all(slices, "wide", split_axis=0, concat_axis=0, tiled=True).astype(F32), axis=0
    ).astype(BF16)
    full = lax.all_to_all(
        jnp.broadcast_to(own[None], slices.shape), "wide", split_axis=0, concat_axis=0, tiled=True
    ).reshape(2 * columns, hidden_units).astype(F32)
    grad_self = full[:columns]
    grad_neighbor = jnp.concatenate([full[columns + 64 :], full[columns : columns + 64]], axis=0)
    return (hidden, grad_self, grad_neighbor)


def solution(mesh):
    return jax.shard_map(
        on_device,
        mesh=mesh,
        in_specs=(
            P("narrow", "wide"),
            P("wide", None, None),
            P("wide", None),
            P("narrow", None),
            P("narrow", None),
            P(("wide", "narrow"), None),
        ),
        out_specs=(P(("wide", "narrow"), None), P("narrow", None), P("narrow", None)),
        check_vma=False,
    )
```

```python
import functools

import jax
import jax.numpy as jnp
from jax import lax
from jax.experimental import pallas as pl
from jax.experimental.pallas import tpu as pltpu
from jax.sharding import PartitionSpec as P

FANOUT = 15
BF16 = jnp.bfloat16
F32 = jnp.float32
VMEM_BYTES = 56 * 1024 * 1024


def activation(value):
    return jax.nn.gelu(value, approximate=True)


def contract_rows(left, right):
    return lax.dot_general(
        left, right, (((0,), (0,)), ((), ())), preferred_element_type=F32
    )


def list_kernel(wide_count, capacity, row_bits, tgt_bits, owner_ref, row_ref, out_ref):
    requests, targets = row_ref.shape
    hi_count = out_ref.shape[0]
    owners = owner_ref[...].reshape(requests, targets)
    masks = jnp.concatenate(
        [jnp.where(owners == w, 1.0, 0.0).astype(BF16) for w in range(wide_count)], axis=0
    )
    lanes = lax.broadcasted_iota(jnp.int32, (targets, targets), 1)
    upper = jnp.where(lax.broadcasted_iota(jnp.int32, (targets, targets), 0) < lanes, 1.0, 0.0)
    within = jnp.dot(masks, upper.astype(BF16), preferred_element_type=F32)
    total = wide_count * requests
    first = lax.broadcasted_iota(jnp.int32, (total, total), 0)
    second = lax.broadcasted_iota(jnp.int32, (total, total), 1)
    lower = jnp.where((second < first) & (second >= first - first % requests), 1.0, 0.0)
    before = jnp.dot(lower.astype(BF16), masks, preferred_element_type=F32)
    offset = jnp.sum(before, axis=1, keepdims=True)
    ranked = masks.astype(F32) * (within + offset)
    slot = jnp.zeros(owners.shape, F32)
    for w in range(wide_count):
        slot = slot + ranked[w * requests : (w + 1) * requests]
    position = owners * capacity + slot.astype(jnp.int32)
    high = position >> 7
    low = position & 127
    target = lax.broadcasted_iota(jnp.int32, owners.shape, 1)
    kind = jnp.where(lax.broadcasted_iota(jnp.int32, owners.shape, 0) == 0, 0, 1)
    code = row_ref[...] | ((target | ((kind | 2) << tgt_bits)) << row_bits)
    parts = [(code & 255).astype(F32), ((code >> 8) & 255).astype(F32), (code >> 16).astype(F32)]
    high_iota = lax.broadcasted_iota(jnp.int32, (hi_count, targets), 0)
    low_iota = lax.broadcasted_iota(jnp.int32, (128, targets), 0)
    sums = jnp.zeros((hi_count, 384), F32)
    for j in range(requests):
        left = jnp.where(high_iota == high[j : j + 1], 1.0, 0.0).astype(BF16)
        hit = low_iota == low[j : j + 1]
        right = jnp.concatenate(
            [jnp.where(hit, part[j : j + 1], 0.0).astype(BF16) for part in parts], axis=0
        )
        sums = sums + lax.dot_general(
            left, right, (((1,), (1,)), ((), ())), preferred_element_type=F32
        )
    out_ref[...] = (sums[:, :128] + sums[:, 128:256] * 256.0 + sums[:, 256:] * 65536.0).astype(
        jnp.int32
    )


def table_kernel(feature_ref, out_ref):
    block = feature_ref[...].astype(F32)
    rest = block[128:]
    count = out_ref.shape[0]
    flat = out_ref.reshape(2 * count, 128)
    flat[pl.ds(0, count, stride=2), :] = jnp.transpose(block[:128])
    flat[pl.ds(1, count, stride=2), :] = jnp.transpose(jnp.concatenate([rest, rest], axis=0))


def owner_kernel(tgt_bits, unroll, rows_ref, place_ref, key_ref, table_ref, weight_ref,
                 keep_ref, send_ref, sums_ref, held, dense):
    source = pl.program_id(0)
    count = pl.num_programs(0)
    capacity = held.shape[0]
    targets = 1 << tgt_bits
    share = targets // 4
    now = source & 1
    flat = held.reshape(2 * capacity, 128)

    def settle(slot):
        dense[slot, :, :128] = flat[pl.ds(0, capacity, stride=2), :].astype(BF16)
        dense[slot, :, 128:] = flat[pl.ds(1, capacity, stride=2), :].astype(BF16)

    @pl.when(source == 0)
    def _():
        def fetch(step, carry):
            for u in range(unroll):
                i = step * unroll + u
                held[i] = table_ref[rows_ref[i]]
            return carry

        lax.fori_loop(0, capacity // unroll, fetch, 0)
        settle(0)

    key = key_ref[0]
    target = key & (targets - 1)
    other = (target // share) ^ place_ref[0]
    piece = 2 * (other & 1) + (other >> 1)
    place = (target & (share - 1)) + piece * share + (key >> tgt_bits) * targets
    place = jnp.where(key >= 0, place, -1)
    row = lax.broadcasted_iota(jnp.int32, (2 * targets, capacity), 0)
    onehot = jnp.where(row == place, 1.0, 0.0).astype(BF16)
    both = jnp.dot(onehot, dense[now], preferred_element_type=F32)
    own = both[:targets]
    mean = both[targets:] / FANOUT
    lane = lax.broadcasted_iota(jnp.int32, (targets, 128), 1)
    mid = jnp.where(lane < 64, own[:, 128:], mean[:, 128:])
    summed = jnp.concatenate([own[:, :128], mid, mean[:, :128]], axis=1).astype(BF16)
    preact = jnp.dot(summed, weight_ref[...], preferred_element_type=F32).astype(BF16)
    sums_ref[:, 0] = summed.reshape(4, share, summed.shape[1])
    keep_ref[:, 0] = preact[: 2 * share].reshape(2, share, preact.shape[1])
    send_ref[:, 0] = preact[2 * share :].reshape(2, share, preact.shape[1])

    ahead = jnp.where(source + 1 < count, source + 1, 0) * capacity
    for i in range(capacity):
        held[i] = table_ref[rows_ref[ahead + i]]
    settle(1 - now)


def swap(value, axis, bit):
    count = lax.axis_size(axis)
    return lax.ppermute(value, axis, [(i, i ^ bit) for i in range(count)])


def on_device(features, owner_of, row_of, w_self, w_neighbor, cotangent):
    wide_count = lax.axis_size("wide")
    targets, requests = row_of.shape
    columns, nodes = features.shape
    hidden_units = w_self.shape[1]
    total = targets * requests
    capacity = max(2, 3 * total // (2 * wide_count))
    row_bits = (nodes - 1).bit_length()
    tgt_bits = (targets - 1).bit_length()
    share = targets // 4

    lists = pl.pallas_call(
        functools.partial(list_kernel, wide_count, capacity, row_bits, tgt_bits),
        out_shape=jax.ShapeDtypeStruct((wide_count * capacity // 128, 128), jnp.int32),
        compiler_params=pltpu.CompilerParams(vmem_limit_bytes=VMEM_BYTES),
        name="lists",
    )(jnp.transpose(owner_of, (1, 2, 0)), jnp.transpose(row_of))
    asked = lax.all_to_all(
        lists.reshape(wide_count, capacity), "wide", split_axis=0, concat_axis=0, tiled=True
    )

    block = nodes // 4
    table = pl.pallas_call(
        table_kernel,
        grid=(nodes // block,),
        in_specs=[pl.BlockSpec((columns, block), lambda i: (0, i))],
        out_specs=pl.BlockSpec((block, 2, 128), lambda i: (i, 0, 0)),
        out_shape=jax.ShapeDtypeStruct((nodes, 2, 128), F32),
        compiler_params=pltpu.CompilerParams(vmem_limit_bytes=VMEM_BYTES),
        cost_estimate=pl.CostEstimate(flops=0, bytes_accessed=24 * 1024 * 1024, transcendentals=0),
        name="table",
    )(features)

    rows = (asked & (nodes - 1)).reshape(wide_count * capacity)
    tail = asked >> row_bits
    keys = jnp.where(tail >= 2 * targets, tail - 2 * targets, -1).reshape(wide_count, 1, capacity)
    weights = jnp.concatenate(
        [w_self[:128], w_self[128:], w_neighbor[128:], w_neighbor[:128]], axis=0
    )
    unroll = next(u for u in (64, 32, 16, 8, 4, 2, 1) if capacity % u == 0)
    place = lax.axis_index("narrow").astype(jnp.int32).reshape(1)
    halves = jax.ShapeDtypeStruct((2, wide_count, share, hidden_units), BF16)
    keep, send, sums = pl.pallas_call(
        functools.partial(owner_kernel, tgt_bits, unroll),
        grid_spec=pltpu.PrefetchScalarGridSpec(
            num_scalar_prefetch=2,
            grid=(wide_count,),
            in_specs=[
                pl.BlockSpec((1, 1, capacity), lambda s, *_: (s, 0, 0)),
                pl.BlockSpec((nodes, 2, 128), lambda s, *_: (0, 0, 0)),
                pl.BlockSpec((2 * columns, hidden_units), lambda s, *_: (0, 0)),
            ],
            out_specs=[
                pl.BlockSpec((2, 1, share, hidden_units), lambda s, *_: (0, s, 0, 0)),
                pl.BlockSpec((2, 1, share, hidden_units), lambda s, *_: (0, s, 0, 0)),
                pl.BlockSpec((4, 1, share, 2 * columns), lambda s, *_: (0, s, 0, 0)),
            ],
            scratch_shapes=[
                pltpu.VMEM((capacity, 2, 128), F32),
                pltpu.VMEM((2, capacity, 256), BF16),
            ],
        ),
        out_shape=[
            halves,
            halves,
            jax.ShapeDtypeStruct((4, wide_count, share, 2 * columns), BF16),
        ],
        compiler_params=pltpu.CompilerParams(vmem_limit_bytes=VMEM_BYTES),
        name="owner",
    )(rows, place, keys, table, weights)

    paired = keep.astype(F32) + swap(send, "narrow", 1).astype(F32)
    quartet = paired[0] + swap(paired[1].astype(BF16), "narrow", 2).astype(F32)
    pieces = lax.all_to_all(
        quartet.astype(BF16), "wide", split_axis=0, concat_axis=0, tiled=True
    )
    preact = jnp.sum(pieces.astype(F32), axis=0)
    value, pullback = jax.vjp(activation, preact)
    hidden = value.astype(BF16)
    slope = pullback(cotangent.astype(F32))[0].astype(BF16)

    slopes = lax.all_to_all(
        jnp.broadcast_to(slope[None], (wide_count, share, hidden_units)),
        "wide", split_axis=0, concat_axis=0, tiled=True,
    )
    across = swap(slopes, "narrow", 2)
    both = jnp.stack([slopes, across])
    beside = swap(both, "narrow", 1)
    rows_per = wide_count * share
    grads = contract_rows(
        sums[:2].reshape(2 * rows_per, 2 * columns), both.reshape(2 * rows_per, hidden_units)
    ) + contract_rows(
        sums[2:].reshape(2 * rows_per, 2 * columns), beside.reshape(2 * rows_per, hidden_units)
    )
    slices = grads.astype(BF16).reshape(wide_count, 2 * columns // wide_count, hidden_units)
    own = jnp.sum(
        lax.all_to_all(slices, "wide", split_axis=0, concat_axis=0, tiled=True).astype(F32), axis=0
    ).astype(BF16)
    full = lax.all_to_all(
        jnp.broadcast_to(own[None], slices.shape), "wide", split_axis=0, concat_axis=0, tiled=True
    ).reshape(2 * columns, hidden_units).astype(F32)
    grad_self = full[:columns]
    grad_neighbor = jnp.concatenate([full[columns + 64 :], full[columns : columns + 64]], axis=0)
    return (hidden, grad_self, grad_neighbor)


def solution(mesh):
    return jax.shard_map(
        on_device,
        mesh=mesh,
        in_specs=(
            P("narrow", "wide"),
            P("wide", None, None),
            P("wide", None),
            P("narrow", None),
            P("narrow", None),
            P(("wide", "narrow"), None),
        ),
        out_specs=(P(("wide", "narrow"), None), P("narrow", None), P("narrow", None)),
        check_vma=False,
    )
```

```python
import functools

import jax
import jax.numpy as jnp
from jax import lax
from jax.experimental import pallas as pl
from jax.experimental.pallas import tpu as pltpu
from jax.sharding import PartitionSpec as P

FANOUT = 15
BF16 = jnp.bfloat16
F32 = jnp.float32
MIB = 1024 * 1024


def activation(value):
    return jax.nn.gelu(value, approximate=True)


def contract_rows(left, right):
    return lax.dot_general(
        left, right, (((0,), (0,)), ((), ())), preferred_element_type=F32
    )


def list_kernel(wide_count, capacity, tgt_bits, owner_ref, row_ref, out_ref):
    requests, targets = row_ref.shape
    hi_count = wide_count * capacity // 128
    owners = owner_ref[...].reshape(requests, targets)
    masks = jnp.concatenate(
        [jnp.where(owners == w, 1.0, 0.0).astype(BF16) for w in range(wide_count)], axis=0
    )
    lanes = lax.broadcasted_iota(jnp.int32, (targets, targets), 1)
    upper = jnp.where(lax.broadcasted_iota(jnp.int32, (targets, targets), 0) < lanes, 1.0, 0.0)
    within = jnp.dot(masks, upper.astype(BF16), preferred_element_type=F32)
    total = wide_count * requests
    first = lax.broadcasted_iota(jnp.int32, (total, total), 0)
    second = lax.broadcasted_iota(jnp.int32, (total, total), 1)
    lower = jnp.where((second < first) & (second >= first - first % requests), 1.0, 0.0)
    before = jnp.dot(lower.astype(BF16), masks, preferred_element_type=F32)
    offset = jnp.sum(before, axis=1, keepdims=True)
    ranked = masks.astype(F32) * (within + offset)
    slot = jnp.zeros(owners.shape, F32)
    for w in range(wide_count):
        slot = slot + ranked[w * requests : (w + 1) * requests]
    position = owners * capacity + slot.astype(jnp.int32)
    high = position >> 7
    low = position & 127
    target = lax.broadcasted_iota(jnp.int32, owners.shape, 1)
    kind = jnp.where(lax.broadcasted_iota(jnp.int32, owners.shape, 0) == 0, 0, 1)
    wanted = row_ref[...]
    key = (target | (kind << tgt_bits)) + 1
    parts = [
        (wanted & 255).astype(F32),
        ((wanted >> 8) | ((key >> 8) << 5)).astype(F32),
        (key & 255).astype(F32),
    ]
    high_iota = lax.broadcasted_iota(jnp.int32, (hi_count, targets), 0)
    low_iota = lax.broadcasted_iota(jnp.int32, (128, targets), 0)
    sums = jnp.zeros((hi_count, 384), F32)
    for j in range(requests):
        left = jnp.where(high_iota == high[j : j + 1], 1.0, 0.0).astype(BF16)
        hit = low_iota == low[j : j + 1]
        right = jnp.concatenate(
            [jnp.where(hit, part[j : j + 1], 0.0).astype(BF16) for part in parts], axis=0
        )
        sums = sums + lax.dot_general(
            left, right, (((1,), (1,)), ((), ())), preferred_element_type=F32
        )
    sums = sums.astype(jnp.int32)
    shared = sums[:, 128:256]
    rows = sums[:, :128] | ((shared & 31) << 8)
    keys = sums[:, 256:] | ((shared >> 5) << 8)
    if capacity % 128:
        out_ref[:hi_count] = rows
        out_ref[hi_count:] = keys
    else:
        each = capacity // 128
        for w in range(wide_count):
            out_ref[2 * w * each : (2 * w + 1) * each] = rows[w * each : (w + 1) * each]
            out_ref[(2 * w + 1) * each : (2 * w + 2) * each] = keys[w * each : (w + 1) * each]


def table_kernel(feature_ref, out_ref):
    block = feature_ref[...].astype(F32)
    rest = block[128:]
    count = out_ref.shape[0]
    flat = out_ref.reshape(2 * count, 128)
    flat[pl.ds(0, count, stride=2), :] = jnp.transpose(block[:128])
    flat[pl.ds(1, count, stride=2), :] = jnp.transpose(jnp.concatenate([rest, rest], axis=0))


def owner_kernel(tgt_bits, unroll, asked_ref, key_ref, table_ref, self_ref, neighbor_ref,
                 keep_ref, send_ref, sums_ref, held, dense, weights):
    step = pl.program_id(0)
    count = pl.num_programs(0)
    capacity = held.shape[0]
    columns = self_ref.shape[0]
    targets = 1 << tgt_bits
    share = targets // 4
    now = step & 1
    flat = held.reshape(2 * capacity, 128)
    mine = lax.axis_index("wide")

    def settle(slot):
        dense[slot, :, :128] = flat[pl.ds(0, capacity, stride=2), :].astype(BF16)
        dense[slot, :, 128:] = flat[pl.ds(1, capacity, stride=2), :].astype(BF16)

    @pl.when(step == 0)
    def _():
        weights[:columns] = self_ref[...]
        weights[columns : columns + 64] = neighbor_ref[128:]
        weights[columns + 64 :] = neighbor_ref[:128]

        def fetch(block, carry):
            for u in range(unroll):
                i = block * unroll + u
                held[i] = table_ref[asked_ref[2 * mine * capacity + i]]
            return carry

        lax.fori_loop(0, capacity // unroll, fetch, 0)
        settle(0)

    key = key_ref[mine ^ step][:, capacity:] - 1
    target = key & (targets - 1)
    other = (target // share) ^ lax.axis_index("narrow")
    piece = 2 * (other & 1) + (other >> 1)
    place = (target & (share - 1)) + piece * share + (key >> tgt_bits) * targets
    place = jnp.where(key >= 0, place, -1)
    row = lax.broadcasted_iota(jnp.int32, (2 * targets, capacity), 0)
    onehot = jnp.where(row == place, 1.0, 0.0).astype(BF16)
    both = jnp.dot(onehot, dense[now], preferred_element_type=F32)
    own = both[:targets]
    mean = both[targets:] / FANOUT
    lane = lax.broadcasted_iota(jnp.int32, (targets, 128), 1)
    mid = jnp.where(lane < 64, own[:, 128:], mean[:, 128:])
    summed = jnp.concatenate([own[:, :128], mid, mean[:, :128]], axis=1).astype(BF16)
    preact = jnp.dot(summed, weights[...], preferred_element_type=F32).astype(BF16)
    sums_ref[:, 0] = summed.reshape(4, share, summed.shape[1])
    keep_ref[:, 0] = preact[: 2 * share].reshape(2, share, preact.shape[1])
    send_ref[:, 0] = preact[2 * share :].reshape(2, share, preact.shape[1])

    ahead = 2 * (mine ^ jnp.where(step + 1 < count, step + 1, 0)) * capacity
    for i in range(capacity):
        held[i] = table_ref[asked_ref[ahead + i]]
    settle(1 - now)


def swap(value, axis, bit):
    count = lax.axis_size(axis)
    return lax.ppermute(value, axis, [(i, i ^ bit) for i in range(count)])


def masks_of(stage_bits):
    count = len(stage_bits)
    return [
        sum(b for i, b in enumerate(stage_bits) if m >> (count - 1 - i) & 1)
        for m in range(1 << count)
    ]


def dims_of(way, bits):
    return [
        0 if axis == "narrow" else bits + 1 - b.bit_length()
        for axis, stage_bits in way
        for b in stage_bits
    ]


def add_across(value, axis, stage_bits):
    masks = masks_of(stage_bits)
    parts = value.reshape((len(masks), -1) + value.shape[-2:])
    came = [swap(parts[i].astype(BF16), axis, masks[i]) for i in range(1, len(masks))]
    return functools.reduce(jnp.add, [part.astype(F32) for part in came], parts[0])


def collect(value, axis, stage_bits):
    parts = [value] + [swap(value, axis, mask) for mask in masks_of(stage_bits)[1:]]
    return jnp.stack(parts)


def on_device(features, owner_of, row_of, w_self, w_neighbor, cotangent):
    wide_count = lax.axis_size("wide")
    targets, requests = row_of.shape
    columns, nodes = features.shape
    hidden_units = w_self.shape[1]
    total = targets * requests
    capacity = max(2, 3 * total // (2 * wide_count))
    tgt_bits = (targets - 1).bit_length()
    share = targets // 4
    half = hidden_units // 2

    lists = pl.pallas_call(
        functools.partial(list_kernel, wide_count, capacity, tgt_bits),
        out_shape=jax.ShapeDtypeStruct((2 * wide_count * capacity // 128, 128), jnp.int32),
        compiler_params=pltpu.CompilerParams(vmem_limit_bytes=32 * MIB),
        name="lists",
    )(jnp.transpose(owner_of, (1, 2, 0)), jnp.transpose(row_of))
    if capacity % 128:
        lists = jnp.transpose(lists.reshape(2, wide_count, capacity), (1, 0, 2))
    asked = lax.all_to_all(
        lists.reshape(wide_count, 2 * capacity), "wide", split_axis=0, concat_axis=0, tiled=True
    )

    block = nodes // 4
    table = pl.pallas_call(
        table_kernel,
        grid=(nodes // block,),
        in_specs=[pl.BlockSpec((columns, block), lambda i: (0, i))],
        out_specs=pl.BlockSpec((block, 2, 128), lambda i: (i, 0, 0)),
        out_shape=jax.ShapeDtypeStruct((nodes, 2, 128), F32),
        compiler_params=pltpu.CompilerParams(vmem_limit_bytes=20 * MIB),
        cost_estimate=pl.CostEstimate(flops=0, bytes_accessed=24 * MIB, transcendentals=0),
        name="table",
    )(features)

    unroll = next(u for u in (64, 32, 16, 8, 4, 2, 1) if capacity % u == 0)
    halves = jax.ShapeDtypeStruct((2, wide_count, share, hidden_units), BF16)
    whole = pl.BlockSpec(memory_space=pltpu.VMEM)
    keep, send, sums = pl.pallas_call(
        functools.partial(owner_kernel, tgt_bits, unroll),
        grid_spec=pltpu.PrefetchScalarGridSpec(
            num_scalar_prefetch=1,
            grid=(wide_count,),
            in_specs=[whole] * 4,
            out_specs=[
                pl.BlockSpec((2, 1, share, hidden_units), lambda s, *_: (0, s, 0, 0)),
                pl.BlockSpec((2, 1, share, hidden_units), lambda s, *_: (0, s, 0, 0)),
                pl.BlockSpec((4, 1, share, 2 * columns), lambda s, *_: (0, s, 0, 0)),
            ],
            scratch_shapes=[
                pltpu.VMEM((capacity, 2, 128), F32),
                pltpu.VMEM((2, capacity, 256), BF16),
                pltpu.VMEM((2 * columns, hidden_units), BF16),
            ],
        ),
        out_shape=[
            halves,
            halves,
            jax.ShapeDtypeStruct((4, wide_count, share, 2 * columns), BF16),
        ],
        compiler_params=pltpu.CompilerParams(vmem_limit_bytes=30 * MIB),
        name="owner",
    )(asked.reshape(-1), asked.reshape(wide_count, 1, 2 * capacity), table, w_self, w_neighbor)

    bits = wide_count.bit_length() - 1
    far = ("narrow", (2,))
    steps = [("wide", (1 << b,)) for b in range(bits)]
    pair = ("wide", (2, 1))
    ways = [[far] + steps, [pair] + steps[2:] + [far]]
    backs = [steps[:1:-1] + [pair, far], steps[:1:-1] + [far, pair]]
    pieces = (2,) * (1 + bits) + (share, hidden_units)
    paired = keep.astype(F32).reshape(pieces) + swap(send, "narrow", 1).astype(F32).reshape(pieces)
    chains = [
        jnp.transpose(paired[..., c * half : (c + 1) * half], dims_of(way, bits) + [bits + 1, bits + 2])
        for c, way in enumerate(ways)
    ]
    for s in range(max(map(len, ways))):
        for c, way in enumerate(ways):
            if s < len(way):
                chains[c] = add_across(chains[c], *way[s])
    preact = jnp.concatenate([chain.reshape(share, half) for chain in chains], axis=1)
    value, pullback = jax.vjp(activation, preact)
    hidden = value.astype(BF16)
    slope = pullback(cotangent.astype(F32))[0].astype(BF16)

    chains = [slope[:, :half], slope[:, half:]]
    for s in range(max(map(len, backs))):
        for c in (1, 0):
            if s < len(backs[c]):
                chains[c] = collect(chains[c], *backs[c][s])
    near = []
    for c, back in enumerate(backs):
        dims = dims_of(back[::-1], bits)
        order = [dims.index(d) for d in range(bits + 1)] + [bits + 1, bits + 2]
        whole_chain = chains[c].reshape((2,) * (1 + bits) + (share, half))
        near.append(jnp.transpose(whole_chain, order).reshape(-1, half))
    beside = [swap(n, "narrow", 1) for n in near]
    rows = 2 * wide_count * share
    ours = sums[:2].reshape(rows, 2 * columns)
    theirs = sums[2:].reshape(rows, 2 * columns)
    grads = contract_rows(ours, jnp.concatenate(near, axis=1)) + contract_rows(
        theirs, jnp.concatenate(beside, axis=1)
    )
    chains = [grads[:columns], grads[columns:]]
    turns = [steps, steps[-1:] + steps[:-1]]
    for s in range(bits):
        for c in range(2):
            mine = chains[c].astype(BF16)
            axis, (bit,) = turns[c][s]
            chains[c] = mine.astype(F32) + swap(mine, axis, bit).astype(F32)
    grad_self, mixed = chains
    grad_neighbor = jnp.concatenate([mixed[columns - 128 :], mixed[: columns - 128]], axis=0)
    return (hidden, grad_self, grad_neighbor)


def solution(mesh):
    return jax.shard_map(
        on_device,
        mesh=mesh,
        in_specs=(
            P("narrow", "wide"),
            P("wide", None, None),
            P("wide", None),
            P("narrow", None),
            P("narrow", None),
            P(("wide", "narrow"), None),
        ),
        out_specs=(P(("wide", "narrow"), None), P("narrow", None), P("narrow", None)),
        check_vma=False,
    )
```

```python
import functools

import jax
import jax.numpy as jnp
from jax import lax
from jax.experimental import pallas as pl
from jax.experimental.pallas import tpu as pltpu
from jax.sharding import PartitionSpec as P

FANOUT = 15
BF16 = jnp.bfloat16
F32 = jnp.float32
MIB = 1024 * 1024


def activation(value):
    return jax.nn.gelu(value, approximate=True)


def contract_rows(left, right):
    return lax.dot_general(
        left, right, (((0,), (0,)), ((), ())), preferred_element_type=F32
    )


def list_kernel(wide_count, capacity, tgt_bits, owner_ref, row_ref, *out_refs):
    requests, targets = row_ref.shape
    hi_count = wide_count * capacity // 128
    owners = owner_ref[...].reshape(requests, targets)
    masks = jnp.concatenate(
        [jnp.where(owners == w, 1.0, 0.0).astype(BF16) for w in range(wide_count)], axis=0
    )
    lanes = lax.broadcasted_iota(jnp.int32, (targets, targets), 1)
    upper = jnp.where(lax.broadcasted_iota(jnp.int32, (targets, targets), 0) < lanes, 1.0, 0.0)
    within = jnp.dot(masks, upper.astype(BF16), preferred_element_type=F32)
    total = wide_count * requests
    first = lax.broadcasted_iota(jnp.int32, (total, total), 0)
    second = lax.broadcasted_iota(jnp.int32, (total, total), 1)
    lower = jnp.where((second < first) & (second >= first - first % requests), 1.0, 0.0)
    before = jnp.dot(lower.astype(BF16), masks, preferred_element_type=F32)
    offset = jnp.sum(before, axis=1, keepdims=True)
    ranked = masks.astype(F32) * (within + offset)
    slot = jnp.zeros(owners.shape, F32)
    for w in range(wide_count):
        slot = slot + ranked[w * requests : (w + 1) * requests]
    apart = owners ^ lax.axis_index("wide")
    turn = (apart & 3) * (wide_count // 4) + (apart >> 2)
    position = turn * capacity + slot.astype(jnp.int32)
    high = (position >> 7) + ((position >> 6) & 1) * hi_count
    low = position & 63
    target = lax.broadcasted_iota(jnp.int32, owners.shape, 1)
    kind = jnp.where(lax.broadcasted_iota(jnp.int32, owners.shape, 0) == 0, 0, 1)
    wanted = row_ref[...]
    key = (target | (kind << tgt_bits)) + 1
    parts = [
        (wanted & 255).astype(F32),
        ((wanted >> 8) | ((key >> 8) << 5)).astype(F32),
        (key & 255).astype(F32),
    ]
    high_iota = lax.broadcasted_iota(jnp.int32, (2 * hi_count, targets), 0)
    low_iota = lax.broadcasted_iota(jnp.int32, (64, targets), 0)
    sums = jnp.zeros((2 * hi_count, 192), F32)
    for j in range(requests):
        left = jnp.where(high_iota == high[j : j + 1], 1.0, 0.0).astype(BF16)
        hit = low_iota == low[j : j + 1]
        right = jnp.concatenate(
            [jnp.where(hit, part[j : j + 1], 0.0).astype(BF16) for part in parts], axis=0
        )
        sums = sums + lax.dot_general(
            left, right, (((1,), (1,)), ((), ())), preferred_element_type=F32
        )
    sums = sums.astype(jnp.int32)
    shared = sums[:, 64:128]
    rows = sums[:, :64] | ((shared & 31) << 8)
    keys = sums[:, 128:] | ((shared >> 5) << 8)
    rows = jnp.concatenate([rows[:hi_count], rows[hi_count:]], axis=1)
    keys = jnp.concatenate([keys[:hi_count], keys[hi_count:]], axis=1)
    if capacity % 128:
        out_refs[0][:hi_count] = rows
        out_refs[0][hi_count:] = keys
    else:
        each = capacity // 128
        for w in range(wide_count):
            out_ref = out_refs[w // (wide_count // 4)]
            at = 2 * (w % (wide_count // 4)) * each
            out_ref[at : at + each] = rows[w * each : (w + 1) * each]
            out_ref[at + each : at + 2 * each] = keys[w * each : (w + 1) * each]


def table_kernel(feature_ref, out_ref):
    block = feature_ref[...].astype(F32)
    rest = block[128:]
    count = out_ref.shape[0]
    flat = out_ref.reshape(2 * count, 128)
    flat[pl.ds(0, count, stride=2), :] = jnp.transpose(block[:128])
    flat[pl.ds(1, count, stride=2), :] = jnp.transpose(jnp.concatenate([rest, rest], axis=0))


def owner_kernel(tgt_bits, unroll, asked_ref, key_ref, table_ref, self_ref, neighbor_ref,
                 keep_ref, send_ref, sums_ref, held, dense, weights):
    step = pl.program_id(0)
    count = pl.num_programs(0)
    capacity = held.shape[0]
    columns = self_ref.shape[0]
    targets = 1 << tgt_bits
    share = targets // 4
    now = step & 1
    flat = held.reshape(2 * capacity, 128)

    def settle(slot):
        dense[slot, :, :128] = flat[pl.ds(0, capacity, stride=2), :].astype(BF16)
        dense[slot, :, 128:] = flat[pl.ds(1, capacity, stride=2), :].astype(BF16)

    @pl.when(step == 0)
    def _():
        weights[:columns] = self_ref[...]
        weights[columns : columns + 64] = neighbor_ref[128:]
        weights[columns + 64 :] = neighbor_ref[:128]

        def fetch(block, carry):
            first = block * unroll
            into = held.at[pl.ds(first, unroll)]
            for u in range(unroll):
                into[u] = table_ref[asked_ref[first + u]]
            return carry

        lax.fori_loop(0, capacity // unroll, fetch, 0)
        settle(0)

    def serve(fetches):
        key = key_ref[step][:, capacity:] - 1
        target = key & (targets - 1)
        other = (target // share) ^ lax.axis_index("narrow")
        piece = 2 * (other & 1) + (other >> 1)
        place = (target & (share - 1)) + piece * share

        def summed_where(wanted, slots):
            row = lax.broadcasted_iota(jnp.int32, (targets, slots), 0)
            onehot = jnp.where(row == jnp.where(wanted, place, -1)[:, :slots], 1.0, 0.0)
            return jnp.dot(onehot.astype(BF16), dense[now, :slots], preferred_element_type=F32)

        own = summed_where((key >= 0) & (key < targets), min(targets, capacity))
        mean = summed_where(key >= targets, capacity) * (1.0 / FANOUT)
        lane = lax.broadcasted_iota(jnp.int32, (targets, 128), 1)
        mid = jnp.where(lane < 64, own[:, 128:], mean[:, 128:])
        summed = jnp.concatenate([own[:, :128], mid, mean[:, :128]], axis=1).astype(BF16)
        preact = jnp.dot(summed, weights[...], preferred_element_type=F32).astype(BF16)
        sums_ref[:, 0] = summed.reshape(4, share, summed.shape[1])
        keep_ref[:, 0] = preact[: 2 * share].reshape(2, share, preact.shape[1])
        send_ref[:, 0] = preact[2 * share :].reshape(2, share, preact.shape[1])
        if fetches:
            ahead = 2 * (step + 1) * capacity
            for i in range(capacity):
                held[i] = table_ref[asked_ref[ahead + i]]
            settle(1 - now)

    pl.when(step + 1 < count)(lambda: serve(True))
    pl.when(step + 1 == count)(lambda: serve(False))


def swap(value, axis, bit):
    count = lax.axis_size(axis)
    return lax.ppermute(value, axis, [(i, i ^ bit) for i in range(count)])


def masks_of(stage_bits):
    count = len(stage_bits)
    return [
        sum(b for i, b in enumerate(stage_bits) if m >> (count - 1 - i) & 1)
        for m in range(1 << count)
    ]


def dims_of(way, bits):
    return [
        0 if axis == "narrow" else bits + 1 - b.bit_length()
        for axis, stage_bits in way
        for b in stage_bits
    ]


def add_across(value, axis, stage_bits):
    masks = masks_of(stage_bits)
    parts = value.reshape((len(masks), -1) + value.shape[-2:])
    came = [swap(parts[i].astype(BF16), axis, masks[i]) for i in range(1, len(masks))]
    return functools.reduce(jnp.add, [part.astype(F32) for part in came], parts[0])


def collect(value, axis, stage_bits):
    parts = [value] + [swap(value, axis, mask) for mask in masks_of(stage_bits)[1:]]
    return jnp.stack(parts)


def add_all(value, axis, stage_bits):
    mine = value.astype(BF16)
    parts = [mine.astype(F32)]
    parts += [swap(mine, axis, mask).astype(F32) for mask in masks_of(stage_bits)[1:]]
    while len(parts) > 1:
        parts = [parts[i] + parts[i + 1] for i in range(0, len(parts), 2)]
    return parts[0]


def on_device(features, owner_of, row_of, w_self, w_neighbor, cotangent):
    wide_count = lax.axis_size("wide")
    targets, requests = row_of.shape
    columns, nodes = features.shape
    hidden_units = w_self.shape[1]
    total = targets * requests
    capacity = max(2, 3 * total // (2 * wide_count))
    tgt_bits = (targets - 1).bit_length()
    share = targets // 4
    half = hidden_units // 2

    block = nodes // 4
    table = pl.pallas_call(
        table_kernel,
        grid=(nodes // block,),
        in_specs=[pl.BlockSpec((columns, block), lambda i: (0, i))],
        out_specs=pl.BlockSpec((block, 2, 128), lambda i: (i, 0, 0)),
        out_shape=jax.ShapeDtypeStruct((nodes, 2, 128), F32),
        compiler_params=pltpu.CompilerParams(vmem_limit_bytes=20 * MIB),
        cost_estimate=pl.CostEstimate(flops=0, bytes_accessed=24 * MIB, transcendentals=0),
        name="table",
    )(features)

    quarter = wide_count // 4 * 2 * capacity // 128
    blocks = [quarter] * 4 if capacity % 128 == 0 else [4 * quarter]
    parts = pl.pallas_call(
        functools.partial(list_kernel, wide_count, capacity, tgt_bits),
        out_shape=[jax.ShapeDtypeStruct((rows, 128), jnp.int32) for rows in blocks],
        compiler_params=pltpu.CompilerParams(vmem_limit_bytes=56 * MIB),
        name="lists",
    )(jnp.transpose(owner_of, (1, 2, 0)), jnp.transpose(row_of))
    if capacity % 128:
        both = jnp.transpose(parts[0].reshape(2, wide_count, capacity), (1, 0, 2))
        parts = list(both.reshape(4, wide_count // 4, 2 * capacity))
    bits = wide_count.bit_length() - 1
    came = [swap(parts[m], "wide", m) for m in range(1, 4)]
    came, table = lax.optimization_barrier((came, table))
    asked = jnp.stack([parts[0]] + came).reshape(4, wide_count // 4, 2 * capacity)
    for b in range(2, bits):
        split = asked.reshape(asked.shape[0], -1, 2, 2 * capacity)
        asked = jnp.concatenate([split[:, :, 0], swap(split[:, :, 1], "wide", 1 << b)], axis=0)

    unroll = next(u for u in (128, 64, 32, 16, 8, 4, 2, 1) if capacity % u == 0)
    halves = jax.ShapeDtypeStruct((2, wide_count, share, hidden_units), BF16)
    whole = pl.BlockSpec(memory_space=pltpu.VMEM)
    keep, send, sums = pl.pallas_call(
        functools.partial(owner_kernel, tgt_bits, unroll),
        grid_spec=pltpu.PrefetchScalarGridSpec(
            num_scalar_prefetch=1,
            grid=(wide_count,),
            in_specs=[whole] * 4,
            out_specs=[
                pl.BlockSpec((2, 1, share, hidden_units), lambda s, *_: (0, s, 0, 0)),
                pl.BlockSpec((2, 1, share, hidden_units), lambda s, *_: (0, s, 0, 0)),
                pl.BlockSpec((4, 1, share, 2 * columns), lambda s, *_: (0, s, 0, 0)),
            ],
            scratch_shapes=[
                pltpu.VMEM((capacity, 2, 128), F32),
                pltpu.VMEM((2, capacity, 256), BF16),
                pltpu.VMEM((2 * columns, hidden_units), BF16),
            ],
        ),
        out_shape=[
            halves,
            halves,
            jax.ShapeDtypeStruct((4, wide_count, share, 2 * columns), BF16),
        ],
        compiler_params=pltpu.CompilerParams(vmem_limit_bytes=30 * MIB),
        name="owner",
    )(asked.reshape(-1), asked.reshape(wide_count, 1, 2 * capacity), table, w_self, w_neighbor)

    far = ("narrow", (2,))
    steps = [("wide", (1 << b,)) for b in range(bits)]
    pair = ("wide", (2, 1))
    ways = [[far] + steps, [pair] + steps[2:] + [far]]
    backs = [steps[:1:-1] + [pair, far], steps[:1:-1] + [far, pair]]
    pieces = (2,) * (1 + bits) + (share, hidden_units)
    paired = keep.astype(F32).reshape(pieces) + swap(send, "narrow", 1).astype(F32).reshape(pieces)
    chains = [
        jnp.transpose(paired[..., c * half : (c + 1) * half], dims_of(way, bits) + [bits + 1, bits + 2])
        for c, way in enumerate(ways)
    ]
    for s in range(max(map(len, ways))):
        for c, way in enumerate(ways):
            if s < len(way):
                chains[c] = add_across(chains[c], *way[s])
    preact = jnp.concatenate([chain.reshape(share, half) for chain in chains], axis=1)
    value, pullback = jax.vjp(activation, preact)
    hidden = value.astype(BF16)
    slope = pullback(cotangent.astype(F32))[0].astype(BF16)

    chains = [slope[:, :half], slope[:, half:]]
    for s in range(max(map(len, backs))):
        for c in (1, 0):
            if s < len(backs[c]):
                chains[c] = collect(chains[c], *backs[c][s])
    near = []
    for c, back in enumerate(backs):
        dims = dims_of(back[::-1], bits)
        order = [dims.index(d) for d in range(bits + 1)] + [bits + 1, bits + 2]
        whole_chain = chains[c].reshape((2,) * (1 + bits) + (share, half))
        near.append(jnp.transpose(whole_chain, order).reshape(-1, half))
    beside = [swap(n, "narrow", 1) for n in near]
    rows = 2 * wide_count * share
    ours = sums[:2].reshape(rows, 2 * columns)
    theirs = sums[2:].reshape(rows, 2 * columns)
    grads = contract_rows(ours, jnp.concatenate(near, axis=1)) + contract_rows(
        theirs, jnp.concatenate(beside, axis=1)
    )
    chains = [grads[:columns], grads[columns:]]
    turns = [[pair] + steps[2:], steps[2:] + [pair]]
    for s in range(len(turns[0])):
        for c in range(2):
            chains[c] = add_all(chains[c], *turns[c][s])
    grad_self, mixed = chains
    grad_neighbor = jnp.concatenate([mixed[columns - 128 :], mixed[: columns - 128]], axis=0)
    return (hidden, grad_self, grad_neighbor)


def solution(mesh):
    return jax.shard_map(
        on_device,
        mesh=mesh,
        in_specs=(
            P("narrow", "wide"),
            P("wide", None, None),
            P("wide", None),
            P("narrow", None),
            P("narrow", None),
            P(("wide", "narrow"), None),
        ),
        out_specs=(P(("wide", "narrow"), None), P("narrow", None), P("narrow", None)),
        check_vma=False,
    )
```

```python
import functools

import jax
import jax.numpy as jnp
from jax import lax
from jax.experimental import pallas as pl
from jax.experimental.pallas import tpu as pltpu
from jax.sharding import PartitionSpec as P

FANOUT = 15
BF16 = jnp.bfloat16
F32 = jnp.float32
MIB = 1024 * 1024


def activation(value):
    return jax.nn.gelu(value, approximate=True)


def contract_rows(left, right):
    return lax.dot_general(
        left, right, (((0,), (0,)), ((), ())), preferred_element_type=F32
    )


def list_kernel(wide_count, capacity, tgt_bits, owner_ref, row_ref, *out_refs):
    requests, targets = row_ref.shape
    hi_count = wide_count * capacity // 128
    owners = owner_ref[...].reshape(requests, targets)
    masks = jnp.concatenate(
        [jnp.where(owners == w, 1.0, 0.0).astype(BF16) for w in range(wide_count)], axis=0
    )
    lanes = lax.broadcasted_iota(jnp.int32, (targets, targets), 1)
    upper = jnp.where(lax.broadcasted_iota(jnp.int32, (targets, targets), 0) < lanes, 1.0, 0.0)
    within = jnp.dot(masks, upper.astype(BF16), preferred_element_type=F32)
    total = wide_count * requests
    first = lax.broadcasted_iota(jnp.int32, (total, total), 0)
    second = lax.broadcasted_iota(jnp.int32, (total, total), 1)
    lower = jnp.where((second < first) & (second >= first - first % requests), 1.0, 0.0)
    before = jnp.dot(lower.astype(BF16), masks, preferred_element_type=F32)
    offset = jnp.sum(before, axis=1, keepdims=True)
    ranked = masks.astype(F32) * (within + offset)
    slot = jnp.zeros(owners.shape, F32)
    for w in range(wide_count):
        slot = slot + ranked[w * requests : (w + 1) * requests]
    apart = owners ^ lax.axis_index("wide")
    turn = (apart & 3) * (wide_count // 4) + (apart >> 2)
    position = turn * capacity + slot.astype(jnp.int32)
    high = (position >> 7) + ((position >> 6) & 1) * hi_count
    low = position & 63
    target = lax.broadcasted_iota(jnp.int32, owners.shape, 1)
    kind = jnp.where(lax.broadcasted_iota(jnp.int32, owners.shape, 0) == 0, 0, 1)
    wanted = row_ref[...]
    key = (target | (kind << tgt_bits)) + 1
    parts = [
        (wanted & 255).astype(F32),
        ((wanted >> 8) | ((key >> 8) << 5)).astype(F32),
        (key & 255).astype(F32),
    ]
    high_iota = lax.broadcasted_iota(jnp.int32, (2 * hi_count, targets), 0)
    low_iota = lax.broadcasted_iota(jnp.int32, (64, targets), 0)
    sums = jnp.zeros((2 * hi_count, 192), F32)
    for j in range(requests):
        left = jnp.where(high_iota == high[j : j + 1], 1.0, 0.0).astype(BF16)
        hit = low_iota == low[j : j + 1]
        right = jnp.concatenate(
            [jnp.where(hit, part[j : j + 1], 0.0).astype(BF16) for part in parts], axis=0
        )
        sums = sums + lax.dot_general(
            left, right, (((1,), (1,)), ((), ())), preferred_element_type=F32
        )
    sums = sums.astype(jnp.int32)
    shared = sums[:, 64:128]
    rows = sums[:, :64] | ((shared & 31) << 8)
    keys = sums[:, 128:] | ((shared >> 5) << 8)
    rows = jnp.concatenate([rows[:hi_count], rows[hi_count:]], axis=1)
    keys = jnp.concatenate([keys[:hi_count], keys[hi_count:]], axis=1)
    if capacity % 128:
        out_refs[0][:hi_count] = rows
        out_refs[0][hi_count:] = keys
    else:
        each = capacity // 128
        for w in range(wide_count):
            out_ref = out_refs[w // (wide_count // 4)]
            at = 2 * (w % (wide_count // 4)) * each
            out_ref[at : at + each] = rows[w * each : (w + 1) * each]
            out_ref[at + each : at + 2 * each] = keys[w * each : (w + 1) * each]


def table_kernel(feature_ref, out_ref):
    block = feature_ref[...].astype(F32)
    rest = block[128:]
    count = out_ref.shape[0]
    flat = out_ref.reshape(2 * count, 128)
    flat[pl.ds(0, count, stride=2), :] = jnp.transpose(block[:128])
    flat[pl.ds(1, count, stride=2), :] = jnp.transpose(jnp.concatenate([rest, rest], axis=0))


def settle(held, into):
    count = held.shape[0]
    flat = held.reshape(2 * count, 128)
    into[:, :128] = flat[pl.ds(0, count, stride=2), :].astype(BF16)
    into[:, 128:] = flat[pl.ds(1, count, stride=2), :].astype(BF16)


def first_kernel(unroll, asked_ref, table_ref, out_ref, held):
    def fetch(block, carry):
        first = block * unroll
        into = held.at[pl.ds(first, unroll)]
        for u in range(unroll):
            into[u] = table_ref[asked_ref[first + u]]
        return carry

    lax.fori_loop(0, held.shape[0] // unroll, fetch, 0)
    settle(held, out_ref)


def owner_kernel(tgt_bits, asked_ref, key_ref, table_ref, first_ref, near_ref, beside_ref, held, dense):
    step = pl.program_id(0)
    count = pl.num_programs(0)
    capacity = held.shape[0]
    targets = 1 << tgt_bits
    share = targets // 4
    now = step & 1

    @pl.when(step == 0)
    def _():
        dense[0] = first_ref[...]

    def serve(fetches):
        key = key_ref[step][:, capacity:] - 1
        target = key & (targets - 1)
        other = (target // share) ^ lax.axis_index("narrow")
        piece = 2 * (other & 1) + (other >> 1)
        place = (target & (share - 1)) + piece * share

        def summed_where(wanted, slots):
            row = lax.broadcasted_iota(jnp.int32, (targets, slots), 0)
            onehot = jnp.where(row == jnp.where(wanted, place, -1)[:, :slots], 1.0, 0.0)
            return jnp.dot(onehot.astype(BF16), dense[now, :slots], preferred_element_type=F32)

        own = summed_where((key >= 0) & (key < targets), min(targets, capacity))
        mean = summed_where(key >= targets, capacity) * (1.0 / FANOUT)
        lane = lax.broadcasted_iota(jnp.int32, (targets, 128), 1)
        mid = jnp.where(lane < 64, own[:, 128:], mean[:, 128:])
        summed = jnp.concatenate([own[:, :128], mid, mean[:, :128]], axis=1).astype(BF16)
        halves = summed.reshape(2, 2, share, summed.shape[1])
        near_ref[:, 0] = halves[0]
        beside_ref[:, 0] = halves[1]
        if fetches:
            ahead = 2 * (step + 1) * capacity
            for i in range(capacity):
                held[i] = table_ref[asked_ref[ahead + i]]
            settle(held, dense.at[1 - now])

    pl.when(step + 1 < count)(lambda: serve(True))
    pl.when(step + 1 == count)(lambda: serve(False))


def swap(value, axis, bit):
    count = lax.axis_size(axis)
    return lax.ppermute(value, axis, [(i, i ^ bit) for i in range(count)])


def masks_of(stage_bits):
    count = len(stage_bits)
    return [
        sum(b for i, b in enumerate(stage_bits) if m >> (count - 1 - i) & 1)
        for m in range(1 << count)
    ]


def dims_of(way, bits):
    return [
        0 if axis == "narrow" else bits + 1 - b.bit_length()
        for axis, stage_bits in way
        for b in stage_bits
    ]


def add_across(value, axis, stage_bits):
    masks = masks_of(stage_bits)
    parts = value.reshape((len(masks), -1) + value.shape[-2:])
    came = [swap(parts[i].astype(BF16), axis, masks[i]) for i in range(1, len(masks))]
    return functools.reduce(jnp.add, [part.astype(F32) for part in came], parts[0])


def collect(value, axis, stage_bits):
    parts = [value] + [swap(value, axis, mask) for mask in masks_of(stage_bits)[1:]]
    return jnp.stack(parts)


def add_all(value, axis, stage_bits):
    mine = value.astype(BF16)
    parts = [mine.astype(F32)]
    parts += [swap(mine, axis, mask).astype(F32) for mask in masks_of(stage_bits)[1:]]
    while len(parts) > 1:
        parts = [parts[i] + parts[i + 1] for i in range(0, len(parts), 2)]
    return parts[0]


def on_device(features, owner_of, row_of, w_self, w_neighbor, cotangent):
    wide_count = lax.axis_size("wide")
    targets, requests = row_of.shape
    columns, nodes = features.shape
    hidden_units = w_self.shape[1]
    total = targets * requests
    capacity = max(2, 3 * total // (2 * wide_count))
    tgt_bits = (targets - 1).bit_length()
    share = targets // 4
    half = hidden_units // 2

    block = nodes // 4
    table = pl.pallas_call(
        table_kernel,
        grid=(nodes // block,),
        in_specs=[pl.BlockSpec((columns, block), lambda i: (0, i))],
        out_specs=pl.BlockSpec((block, 2, 128), lambda i: (i, 0, 0)),
        out_shape=jax.ShapeDtypeStruct((nodes, 2, 128), F32),
        compiler_params=pltpu.CompilerParams(vmem_limit_bytes=20 * MIB),
        cost_estimate=pl.CostEstimate(flops=0, bytes_accessed=24 * MIB, transcendentals=0),
        name="table",
    )(features)

    quarter = wide_count // 4 * 2 * capacity // 128
    blocks = [quarter] * 4 if capacity % 128 == 0 else [4 * quarter]
    parts = pl.pallas_call(
        functools.partial(list_kernel, wide_count, capacity, tgt_bits),
        out_shape=[jax.ShapeDtypeStruct((rows, 128), jnp.int32) for rows in blocks],
        compiler_params=pltpu.CompilerParams(vmem_limit_bytes=56 * MIB),
        name="lists",
    )(jnp.transpose(owner_of, (1, 2, 0)), jnp.transpose(row_of))
    if capacity % 128:
        both = jnp.transpose(parts[0].reshape(2, wide_count, capacity), (1, 0, 2))
        parts = list(both.reshape(4, wide_count // 4, 2 * capacity))
    bits = wide_count.bit_length() - 1
    weights = jnp.concatenate(
        [w_self, w_neighbor[128:], w_neighbor[:128]], axis=0
    )
    came = [swap(parts[m], "wide", m) for m in range(1, 4)]
    came, table = lax.optimization_barrier((came, table))
    asked = jnp.stack([parts[0]] + came).reshape(4, wide_count // 4, 2 * capacity)
    for b in range(2, bits):
        split = asked.reshape(asked.shape[0], -1, 2, 2 * capacity)
        asked = jnp.concatenate([split[:, :, 0], swap(split[:, :, 1], "wide", 1 << b)], axis=0)

    unroll = next(u for u in (128, 64, 32, 16, 8, 4, 2, 1) if capacity % u == 0)
    whole = pl.BlockSpec(memory_space=pltpu.VMEM)
    first = pl.pallas_call(
        functools.partial(first_kernel, unroll),
        grid_spec=pltpu.PrefetchScalarGridSpec(
            num_scalar_prefetch=1,
            grid=(1,),
            in_specs=[whole],
            out_specs=whole,
            scratch_shapes=[pltpu.VMEM((capacity, 2, 128), F32)],
        ),
        out_shape=jax.ShapeDtypeStruct((capacity, 256), BF16),
        compiler_params=pltpu.CompilerParams(vmem_limit_bytes=10 * MIB),
        cost_estimate=pl.CostEstimate(flops=0, bytes_accessed=4 * MIB, transcendentals=0),
        name="first",
    )(parts[0].reshape(-1), table)
    half_sums = (2, wide_count, share, 2 * columns)
    near_sums, beside_sums = pl.pallas_call(
        functools.partial(owner_kernel, tgt_bits),
        grid_spec=pltpu.PrefetchScalarGridSpec(
            num_scalar_prefetch=1,
            grid=(wide_count,),
            in_specs=[whole] * 3,
            out_specs=[
                pl.BlockSpec((2, 1, share, 2 * columns), lambda s, *_: (0, s, 0, 0))
            ] * 2,
            scratch_shapes=[
                pltpu.VMEM((capacity, 2, 128), F32),
                pltpu.VMEM((2, capacity, 256), BF16),
            ],
        ),
        out_shape=[jax.ShapeDtypeStruct(half_sums, BF16)] * 2,
        compiler_params=pltpu.CompilerParams(vmem_limit_bytes=30 * MIB),
        name="owner",
    )(asked.reshape(-1), asked.reshape(wide_count, 1, 2 * capacity), table, first)
    rows = 2 * wide_count * share
    ours = near_sums.reshape(rows, 2 * columns)
    theirs = beside_sums.reshape(rows, 2 * columns)
    far = ("narrow", (2,))
    steps = [("wide", (1 << b,)) for b in range(bits)]
    pair = ("wide", (2, 1))
    ways = [[far] + steps, [pair, far] + steps[2:]]
    backs = [steps[:1:-1] + [pair, far], steps[:1:-1] + [far, pair]]
    pieces = (2,) * (1 + bits) + (share, half)
    chains = []
    for c, way in enumerate(ways):
        columns_of = weights[:, c * half : (c + 1) * half]
        send = jnp.dot(theirs, columns_of, preferred_element_type=F32).astype(BF16)
        keep = lax.optimization_barrier(jnp.dot(ours, columns_of, preferred_element_type=F32))
        paired = keep.reshape(pieces) + swap(send, "narrow", 1).reshape(pieces)
        chains.append(jnp.transpose(paired, dims_of(way, bits) + [bits + 1, bits + 2]))
    for s in range(max(map(len, ways))):
        for c in (0, 1):
            if s < len(ways[c]):
                chains[c] = add_across(chains[c], *ways[c][s])
    preact = jnp.concatenate([chain.reshape(share, half) for chain in chains], axis=1)
    value, pullback = jax.vjp(activation, preact)
    hidden = value.astype(BF16)
    slope = pullback(cotangent.astype(F32))[0].astype(BF16)

    chains = [slope[:, :half], slope[:, half:]]
    for s in range(max(map(len, backs))):
        for c in (1, 0):
            if s < len(backs[c]):
                chains[c] = collect(chains[c], *backs[c][s])
    near = []
    for c, back in enumerate(backs):
        dims = dims_of(back[::-1], bits)
        order = [dims.index(d) for d in range(bits + 1)] + [bits + 1, bits + 2]
        whole_chain = chains[c].reshape((2,) * (1 + bits) + (share, half))
        near.append(jnp.transpose(whole_chain, order).reshape(-1, half))
    beside = [swap(n, "narrow", 1) for n in near]
    grads = contract_rows(ours, jnp.concatenate(near, axis=1)) + contract_rows(
        theirs, jnp.concatenate(beside, axis=1)
    )
    chains = [grads[:columns], grads[columns:]]
    turns = [[pair] + steps[2:], steps[2:] + [pair]]
    for s in range(len(turns[0])):
        for c in (0, 1):
            chains[c] = add_all(chains[c], *turns[c][s])
    grad_self, mixed = chains
    grad_neighbor = jnp.concatenate([mixed[columns - 128 :], mixed[: columns - 128]], axis=0)
    return (hidden, grad_self, grad_neighbor)


def solution(mesh):
    return jax.shard_map(
        on_device,
        mesh=mesh,
        in_specs=(
            P("narrow", "wide"),
            P("wide", None, None),
            P("wide", None),
            P("narrow", None),
            P("narrow", None),
            P(("wide", "narrow"), None),
        ),
        out_specs=(P(("wide", "narrow"), None), P("narrow", None), P("narrow", None)),
        check_vma=False,
    )
```

```python
import functools

import jax
import jax.numpy as jnp
from jax import lax
from jax.experimental import pallas as pl
from jax.experimental.pallas import tpu as pltpu
from jax.sharding import PartitionSpec as P

FANOUT = 15
BF16 = jnp.bfloat16
F32 = jnp.float32
MIB = 1024 * 1024


def activation(value):
    return jax.nn.gelu(value, approximate=True)


def contract_rows(left, right):
    return lax.dot_general(
        left, right, (((0,), (0,)), ((), ())), preferred_element_type=F32
    )


def list_kernel(wide_count, capacity, tgt_bits, owner_ref, row_ref, *out_refs):
    requests, targets = row_ref.shape
    hi_count = wide_count * capacity // 128
    owners = owner_ref[...].reshape(requests, targets)
    masks = jnp.concatenate(
        [jnp.where(owners == w, 1.0, 0.0).astype(BF16) for w in range(wide_count)], axis=0
    )
    lanes = lax.broadcasted_iota(jnp.int32, (targets, targets), 1)
    upper = jnp.where(lax.broadcasted_iota(jnp.int32, (targets, targets), 0) < lanes, 1.0, 0.0)
    within = jnp.dot(masks, upper.astype(BF16), preferred_element_type=F32)
    total = wide_count * requests
    first = lax.broadcasted_iota(jnp.int32, (total, total), 0)
    second = lax.broadcasted_iota(jnp.int32, (total, total), 1)
    lower = jnp.where((second < first) & (second >= first - first % requests), 1.0, 0.0)
    before = jnp.dot(lower.astype(BF16), masks, preferred_element_type=F32)
    offset = jnp.sum(before, axis=1, keepdims=True)
    ranked = masks.astype(F32) * (within + offset)
    slot = jnp.zeros(owners.shape, F32)
    for w in range(wide_count):
        slot = slot + ranked[w * requests : (w + 1) * requests]
    apart = owners ^ lax.axis_index("wide")
    turn = (apart & 3) * (wide_count // 4) + (apart >> 2)
    position = turn * capacity + slot.astype(jnp.int32)
    high = (position >> 7) + ((position >> 6) & 1) * hi_count
    low = position & 63
    target = lax.broadcasted_iota(jnp.int32, owners.shape, 1)
    kind = jnp.where(lax.broadcasted_iota(jnp.int32, owners.shape, 0) == 0, 0, 1)
    wanted = row_ref[...]
    key = (target | (kind << tgt_bits)) + 1
    parts = [
        (wanted & 255).astype(F32),
        ((wanted >> 8) | ((key >> 8) << 5)).astype(F32),
        (key & 255).astype(F32),
    ]
    high_iota = lax.broadcasted_iota(jnp.int32, (2 * hi_count, targets), 0)
    low_iota = lax.broadcasted_iota(jnp.int32, (64, targets), 0)
    sums = jnp.zeros((2 * hi_count, 192), F32)
    for j in range(requests):
        left = jnp.where(high_iota == high[j : j + 1], 1.0, 0.0).astype(BF16)
        hit = low_iota == low[j : j + 1]
        right = jnp.concatenate(
            [jnp.where(hit, part[j : j + 1], 0.0).astype(BF16) for part in parts], axis=0
        )
        sums = sums + lax.dot_general(
            left, right, (((1,), (1,)), ((), ())), preferred_element_type=F32
        )
    sums = sums.astype(jnp.int32)
    shared = sums[:, 64:128]
    rows = sums[:, :64] | ((shared & 31) << 8)
    keys = sums[:, 128:] | ((shared >> 5) << 8)
    rows = jnp.concatenate([rows[:hi_count], rows[hi_count:]], axis=1)
    keys = jnp.concatenate([keys[:hi_count], keys[hi_count:]], axis=1)
    if capacity % 128:
        out_refs[0][:hi_count] = rows
        out_refs[0][hi_count:] = keys
    else:
        each = capacity // 128
        for w in range(wide_count):
            out_ref = out_refs[w // (wide_count // 4)]
            at = 2 * (w % (wide_count // 4)) * each
            out_ref[at : at + each] = rows[w * each : (w + 1) * each]
            out_ref[at + each : at + 2 * each] = keys[w * each : (w + 1) * each]


def table_kernel(feature_ref, out_ref):
    block = feature_ref[...].astype(F32)
    rest = block[128:]
    count = out_ref.shape[0]
    flat = out_ref.reshape(2 * count, 128)
    flat[pl.ds(0, count, stride=2), :] = jnp.transpose(block[:128])
    flat[pl.ds(1, count, stride=2), :] = jnp.transpose(jnp.concatenate([rest, rest], axis=0))


def settle(held, into):
    count = held.shape[0]
    flat = held.reshape(2 * count, 128)
    into[:, :128] = flat[pl.ds(0, count, stride=2), :].astype(BF16)
    into[:, 128:] = flat[pl.ds(1, count, stride=2), :].astype(BF16)


def first_kernel(unroll, asked_ref, table_ref, out_ref, held):
    def fetch(block, carry):
        first = block * unroll
        into = held.at[pl.ds(first, unroll)]
        for u in range(unroll):
            into[u] = table_ref[asked_ref[first + u]]
        return carry

    lax.fori_loop(0, held.shape[0] // unroll, fetch, 0)
    settle(held, out_ref)


def owner_kernel(tgt_bits, asked_ref, key_ref, table_ref, first_ref, near_ref, beside_ref, held, dense):
    step = pl.program_id(0)
    count = pl.num_programs(0)
    capacity = held.shape[0]
    targets = 1 << tgt_bits
    share = targets // 4
    now = step & 1

    @pl.when(step == 0)
    def _():
        dense[0] = first_ref[...]

    def serve(fetches):
        key = key_ref[step][:, capacity:] - 1
        target = key & (targets - 1)
        other = (target // share) ^ lax.axis_index("narrow")
        piece = 2 * (other & 1) + (other >> 1)
        place = (target & (share - 1)) + piece * share

        def summed_where(wanted, slots):
            row = lax.broadcasted_iota(jnp.int32, (targets, slots), 0)
            onehot = jnp.where(row == jnp.where(wanted, place, -1)[:, :slots], 1.0, 0.0)
            return jnp.dot(onehot.astype(BF16), dense[now, :slots], preferred_element_type=F32)

        own = summed_where((key >= 0) & (key < targets), min(targets, capacity))
        mean = summed_where(key >= targets, capacity) * (1.0 / FANOUT)
        lane = lax.broadcasted_iota(jnp.int32, (targets, 128), 1)
        mid = jnp.where(lane < 64, own[:, 128:], mean[:, 128:])
        summed = jnp.concatenate([own[:, :128], mid, mean[:, :128]], axis=1).astype(BF16)
        halves = summed.reshape(2, 2, share, summed.shape[1])
        near_ref[:, 0] = halves[0]
        beside_ref[:, 0] = halves[1]
        if fetches:
            ahead = 2 * (step + 1) * capacity
            for i in range(capacity):
                held[i] = table_ref[asked_ref[ahead + i]]
            settle(held, dense.at[1 - now])

    pl.when(step + 1 < count)(lambda: serve(True))
    pl.when(step + 1 == count)(lambda: serve(False))


def swap(value, axis, bit):
    count = lax.axis_size(axis)
    return lax.ppermute(value, axis, [(i, i ^ bit) for i in range(count)])


def masks_of(stage_bits):
    count = len(stage_bits)
    return [
        sum(b for i, b in enumerate(stage_bits) if m >> (count - 1 - i) & 1)
        for m in range(1 << count)
    ]


def dims_of(way, bits):
    return [
        0 if axis == "narrow" else bits + 1 - b.bit_length()
        for axis, stage_bits in way
        for b in stage_bits
    ]


def add_across(value, axis, stage_bits):
    masks = masks_of(stage_bits)
    parts = value.reshape((len(masks), -1) + value.shape[-2:])
    came = [swap(parts[i].astype(BF16), axis, masks[i]) for i in range(1, len(masks))]
    return functools.reduce(jnp.add, [part.astype(F32) for part in came], parts[0])


def collect(value, axis, stage_bits):
    parts = [value] + [swap(value, axis, mask) for mask in masks_of(stage_bits)[1:]]
    return jnp.stack(parts)


def add_all(value, axis, stage_bits):
    mine = value.astype(BF16)
    parts = [mine.astype(F32)]
    parts += [swap(mine, axis, mask).astype(F32) for mask in masks_of(stage_bits)[1:]]
    while len(parts) > 1:
        parts = [parts[i] + parts[i + 1] for i in range(0, len(parts), 2)]
    return parts[0]


def on_device(features, owner_of, row_of, w_self, w_neighbor, cotangent):
    wide_count = lax.axis_size("wide")
    targets, requests = row_of.shape
    columns, nodes = features.shape
    hidden_units = w_self.shape[1]
    total = targets * requests
    capacity = max(2, 3 * total // (2 * wide_count))
    tgt_bits = (targets - 1).bit_length()
    share = targets // 4
    half = hidden_units // 2

    block = nodes // 4
    table = pl.pallas_call(
        table_kernel,
        grid=(nodes // block,),
        in_specs=[pl.BlockSpec((columns, block), lambda i: (0, i))],
        out_specs=pl.BlockSpec((block, 2, 128), lambda i: (i, 0, 0)),
        out_shape=jax.ShapeDtypeStruct((nodes, 2, 128), F32),
        compiler_params=pltpu.CompilerParams(vmem_limit_bytes=20 * MIB),
        cost_estimate=pl.CostEstimate(flops=0, bytes_accessed=24 * MIB, transcendentals=0),
        name="table",
    )(features)

    quarter = wide_count // 4 * 2 * capacity // 128
    blocks = [quarter] * 4 if capacity % 128 == 0 else [4 * quarter]
    parts = pl.pallas_call(
        functools.partial(list_kernel, wide_count, capacity, tgt_bits),
        out_shape=[jax.ShapeDtypeStruct((rows, 128), jnp.int32) for rows in blocks],
        compiler_params=pltpu.CompilerParams(vmem_limit_bytes=56 * MIB),
        name="lists",
    )(jnp.transpose(owner_of, (1, 2, 0)), jnp.transpose(row_of))
    if capacity % 128:
        both = jnp.transpose(parts[0].reshape(2, wide_count, capacity), (1, 0, 2))
        parts = list(both.reshape(4, wide_count // 4, 2 * capacity))
    bits = wide_count.bit_length() - 1
    weights = jnp.concatenate(
        [w_self, w_neighbor[128:], w_neighbor[:128]], axis=0
    )
    came = [swap(parts[m], "wide", m) for m in range(1, 4)]
    came, table = lax.optimization_barrier((came, table))
    asked = jnp.stack([parts[0]] + came).reshape(4, wide_count // 4, 2 * capacity)
    for b in range(2, bits):
        split = asked.reshape(asked.shape[0], -1, 2, 2 * capacity)
        asked = jnp.concatenate([split[:, :, 0], swap(split[:, :, 1], "wide", 1 << b)], axis=0)

    unroll = next(u for u in (128, 64, 32, 16, 8, 4, 2, 1) if capacity % u == 0)
    whole = pl.BlockSpec(memory_space=pltpu.VMEM)
    first = pl.pallas_call(
        functools.partial(first_kernel, unroll),
        grid_spec=pltpu.PrefetchScalarGridSpec(
            num_scalar_prefetch=1,
            grid=(1,),
            in_specs=[whole],
            out_specs=whole,
            scratch_shapes=[pltpu.VMEM((capacity, 2, 128), F32)],
        ),
        out_shape=jax.ShapeDtypeStruct((capacity, 256), BF16),
        compiler_params=pltpu.CompilerParams(vmem_limit_bytes=10 * MIB),
        cost_estimate=pl.CostEstimate(flops=0, bytes_accessed=4 * MIB, transcendentals=0),
        name="first",
    )(parts[0].reshape(-1), table)
    half_sums = (2, wide_count, share, 2 * columns)
    near_sums, beside_sums = pl.pallas_call(
        functools.partial(owner_kernel, tgt_bits),
        grid_spec=pltpu.PrefetchScalarGridSpec(
            num_scalar_prefetch=1,
            grid=(wide_count,),
            in_specs=[whole] * 3,
            out_specs=[
                pl.BlockSpec((2, 1, share, 2 * columns), lambda s, *_: (0, s, 0, 0))
            ] * 2,
            scratch_shapes=[
                pltpu.VMEM((capacity, 2, 128), F32),
                pltpu.VMEM((2, capacity, 256), BF16),
            ],
        ),
        out_shape=[jax.ShapeDtypeStruct(half_sums, BF16)] * 2,
        compiler_params=pltpu.CompilerParams(vmem_limit_bytes=30 * MIB),
        name="owner",
    )(asked.reshape(-1), asked.reshape(wide_count, 1, 2 * capacity), table, first)
    rows = 2 * wide_count * share
    ours = near_sums.reshape(rows, 2 * columns)
    theirs = beside_sums.reshape(rows, 2 * columns)
    far = ("narrow", (2,))
    steps = [("wide", (1 << b,)) for b in range(bits)]
    pair = ("wide", (2, 1))
    ways = [[far] + steps, [pair, far] + steps[2:]]
    backs = [steps[:1:-1] + [pair, far], steps[:1:-1] + [far, pair]]
    pieces = (2,) * (1 + bits) + (share, half)
    chains = []
    for c, way in enumerate(ways):
        columns_of = weights[:, c * half : (c + 1) * half]
        send = jnp.dot(theirs, columns_of, preferred_element_type=F32).astype(BF16)
        keep = lax.optimization_barrier(jnp.dot(ours, columns_of, preferred_element_type=F32))
        paired = keep.reshape(pieces) + swap(send, "narrow", 1).reshape(pieces)
        chains.append(jnp.transpose(paired, dims_of(way, bits) + [bits + 1, bits + 2]))
    for s in range(max(map(len, ways))):
        for c in (0, 1):
            if s < len(ways[c]):
                chains[c] = add_across(chains[c], *ways[c][s])
    preact = jnp.concatenate([chain.reshape(share, half) for chain in chains], axis=1)
    value, pullback = jax.vjp(activation, preact)
    hidden = value.astype(BF16)
    slope = pullback(cotangent.astype(F32))[0].astype(BF16)

    chains = [slope[:, :half], slope[:, half:]]
    for s in range(max(map(len, backs))):
        for c in (1, 0):
            if s < len(backs[c]):
                chains[c] = collect(chains[c], *backs[c][s])
    near = []
    for c, back in enumerate(backs):
        dims = dims_of(back[::-1], bits)
        order = [dims.index(d) for d in range(bits + 1)] + [bits + 1, bits + 2]
        whole_chain = chains[c].reshape((2,) * (1 + bits) + (share, half))
        near.append(jnp.transpose(whole_chain, order).reshape(-1, half))
    beside = [swap(n, "narrow", 1) for n in near]
    grads = contract_rows(ours, jnp.concatenate(near, axis=1)) + contract_rows(
        theirs, jnp.concatenate(beside, axis=1)
    )
    chains = [grads[:columns], grads[columns:]]
    turns = [steps, steps[1:] + steps[:1]]
    for s in range(len(turns[0])):
        for c in (0, 1):
            chains[c] = add_all(chains[c], *turns[c][s])
    grad_self, mixed = chains
    grad_neighbor = jnp.concatenate([mixed[columns - 128 :], mixed[: columns - 128]], axis=0)
    return (hidden, grad_self, grad_neighbor)


def solution(mesh):
    return jax.shard_map(
        on_device,
        mesh=mesh,
        in_specs=(
            P("narrow", "wide"),
            P("wide", None, None),
            P("wide", None),
            P("narrow", None),
            P("narrow", None),
            P(("wide", "narrow"), None),
        ),
        out_specs=(P(("wide", "narrow"), None), P("narrow", None), P("narrow", None)),
        check_vma=False,
    )
```

```python
import functools

import jax
import jax.numpy as jnp
from jax import lax
from jax.experimental import pallas as pl
from jax.experimental.pallas import tpu as pltpu
from jax.sharding import PartitionSpec as P

FANOUT = 15
BF16 = jnp.bfloat16
F32 = jnp.float32
MIB = 1024 * 1024


def activation(value):
    return jax.nn.gelu(value, approximate=True)


def contract_rows(left, right):
    return lax.dot_general(
        left, right, (((0,), (0,)), ((), ())), preferred_element_type=F32
    )


def list_kernel(wide_count, capacity, tgt_bits, owner_ref, row_ref, *out_refs):
    requests, targets = row_ref.shape
    hi_count = wide_count * capacity // 128
    owners = owner_ref[...].reshape(requests, targets)
    masks = jnp.concatenate(
        [jnp.where(owners == w, 1.0, 0.0).astype(BF16) for w in range(wide_count)], axis=0
    )
    lanes = lax.broadcasted_iota(jnp.int32, (targets, targets), 1)
    upper = jnp.where(lax.broadcasted_iota(jnp.int32, (targets, targets), 0) < lanes, 1.0, 0.0)
    within = jnp.dot(masks, upper.astype(BF16), preferred_element_type=F32)
    total = wide_count * requests
    first = lax.broadcasted_iota(jnp.int32, (total, total), 0)
    second = lax.broadcasted_iota(jnp.int32, (total, total), 1)
    lower = jnp.where((second < first) & (second >= first - first % requests), 1.0, 0.0)
    before = jnp.dot(lower.astype(BF16), masks, preferred_element_type=F32)
    offset = jnp.sum(before, axis=1, keepdims=True)
    ranked = masks.astype(F32) * (within + offset)
    slot = jnp.zeros(owners.shape, F32)
    for w in range(wide_count):
        slot = slot + ranked[w * requests : (w + 1) * requests]
    apart = owners ^ lax.axis_index("wide")
    turn = (apart & 3) * (wide_count // 4) + (apart >> 2)
    position = turn * capacity + slot.astype(jnp.int32)
    high = (position >> 7) + ((position >> 6) & 1) * hi_count
    low = position & 63
    target = lax.broadcasted_iota(jnp.int32, owners.shape, 1)
    kind = jnp.where(lax.broadcasted_iota(jnp.int32, owners.shape, 0) == 0, 0, 1)
    wanted = row_ref[...]
    key = (target | (kind << tgt_bits)) + 1
    parts = [
        (wanted & 255).astype(F32),
        ((wanted >> 8) | ((key >> 8) << 5)).astype(F32),
        (key & 255).astype(F32),
    ]
    high_iota = lax.broadcasted_iota(jnp.int32, (2 * hi_count, targets), 0)
    low_iota = lax.broadcasted_iota(jnp.int32, (64, targets), 0)
    sums = jnp.zeros((2 * hi_count, 192), F32)
    for j in range(requests):
        left = jnp.where(high_iota == high[j : j + 1], 1.0, 0.0).astype(BF16)
        hit = low_iota == low[j : j + 1]
        right = jnp.concatenate(
            [jnp.where(hit, part[j : j + 1], 0.0).astype(BF16) for part in parts], axis=0
        )
        sums = sums + lax.dot_general(
            left, right, (((1,), (1,)), ((), ())), preferred_element_type=F32
        )
    sums = sums.astype(jnp.int32)
    shared = sums[:, 64:128]
    rows = sums[:, :64] | ((shared & 31) << 8)
    keys = sums[:, 128:] | ((shared >> 5) << 8)
    rows = jnp.concatenate([rows[:hi_count], rows[hi_count:]], axis=1)
    keys = jnp.concatenate([keys[:hi_count], keys[hi_count:]], axis=1)
    if capacity % 128:
        out_refs[0][:hi_count] = rows
        out_refs[0][hi_count:] = keys
    else:
        each = capacity // 128
        for w in range(wide_count):
            out_ref = out_refs[w // (wide_count // 4)]
            at = 2 * (w % (wide_count // 4)) * each
            out_ref[at : at + each] = rows[w * each : (w + 1) * each]
            out_ref[at + each : at + 2 * each] = keys[w * each : (w + 1) * each]


def table_kernel(feature_ref, out_ref):
    block = feature_ref[...].astype(F32)
    rest = block[128:]
    count = out_ref.shape[0]
    flat = out_ref.reshape(2 * count, 128)
    flat[pl.ds(0, count, stride=2), :] = jnp.transpose(block[:128])
    flat[pl.ds(1, count, stride=2), :] = jnp.transpose(jnp.concatenate([rest, rest], axis=0))


def settle(held, into):
    count = held.shape[0]
    flat = held.reshape(2 * count, 128)
    into[:, :128] = flat[pl.ds(0, count, stride=2), :].astype(BF16)
    into[:, 128:] = flat[pl.ds(1, count, stride=2), :].astype(BF16)


def first_kernel(unroll, asked_ref, table_ref, out_ref, held):
    def fetch(block, carry):
        first = block * unroll
        into = held.at[pl.ds(first, unroll)]
        for u in range(unroll):
            into[u] = table_ref[asked_ref[first + u]]
        return carry

    lax.fori_loop(0, held.shape[0] // unroll, fetch, 0)
    settle(held, out_ref)


def owner_kernel(tgt_bits, asked_ref, key_ref, table_ref, first_ref, near_ref, beside_ref, held, dense):
    step = pl.program_id(0)
    count = pl.num_programs(0)
    capacity = held.shape[0]
    targets = 1 << tgt_bits
    share = targets // 4
    now = step & 1

    @pl.when(step == 0)
    def _():
        dense[0] = first_ref[...]

    def serve(fetches):
        key = key_ref[step][:, capacity:] - 1
        target = key & (targets - 1)
        other = (target // share) ^ lax.axis_index("narrow")
        piece = 2 * (other & 1) + (other >> 1)
        place = (target & (share - 1)) + piece * share

        def summed_where(wanted, slots):
            row = lax.broadcasted_iota(jnp.int32, (targets, slots), 0)
            onehot = jnp.where(row == jnp.where(wanted, place, -1)[:, :slots], 1.0, 0.0)
            return jnp.dot(onehot.astype(BF16), dense[now, :slots], preferred_element_type=F32)

        own = summed_where((key >= 0) & (key < targets), min(targets, capacity))
        mean = summed_where(key >= targets, capacity) * (1.0 / FANOUT)
        lane = lax.broadcasted_iota(jnp.int32, (targets, 128), 1)
        mid = jnp.where(lane < 64, own[:, 128:], mean[:, 128:])
        summed = jnp.concatenate([own[:, :128], mid, mean[:, :128]], axis=1).astype(BF16)
        halves = summed.reshape(2, 2, share, summed.shape[1])
        near_ref[:, 0] = halves[0]
        beside_ref[:, 0] = halves[1]
        if fetches:
            ahead = 2 * (step + 1) * capacity
            for i in range(capacity):
                held[i] = table_ref[asked_ref[ahead + i]]
            settle(held, dense.at[1 - now])

    pl.when(step + 1 < count)(lambda: serve(True))
    pl.when(step + 1 == count)(lambda: serve(False))


def swap(value, axis, bit):
    count = lax.axis_size(axis)
    return lax.ppermute(value, axis, [(i, i ^ bit) for i in range(count)])


def masks_of(stage_bits):
    count = len(stage_bits)
    return [
        sum(b for i, b in enumerate(stage_bits) if m >> (count - 1 - i) & 1)
        for m in range(1 << count)
    ]


def dims_of(way, bits):
    return [
        0 if axis == "narrow" else bits + 1 - b.bit_length()
        for axis, stage_bits in way
        for b in stage_bits
    ]


def add_across(value, axis, stage_bits):
    masks = masks_of(stage_bits)
    parts = value.reshape((len(masks), -1) + value.shape[-2:])
    came = [swap(parts[i].astype(BF16), axis, masks[i]) for i in range(1, len(masks))]
    return functools.reduce(jnp.add, [part.astype(F32) for part in came], parts[0])


def collect(value, axis, stage_bits):
    parts = [value] + [swap(value, axis, mask) for mask in masks_of(stage_bits)[1:]]
    return jnp.stack(parts)


def add_all(value, axis, stage_bits):
    mine = value.astype(BF16)
    parts = [mine.astype(F32)]
    parts += [swap(mine, axis, mask).astype(F32) for mask in masks_of(stage_bits)[1:]]
    while len(parts) > 1:
        parts = [parts[i] + parts[i + 1] for i in range(0, len(parts), 2)]
    return parts[0]


def on_device(features, owner_of, row_of, w_self, w_neighbor, cotangent):
    wide_count = lax.axis_size("wide")
    targets, requests = row_of.shape
    columns, nodes = features.shape
    hidden_units = w_self.shape[1]
    total = targets * requests
    capacity = max(2, 3 * total // (2 * wide_count))
    tgt_bits = (targets - 1).bit_length()
    share = targets // 4
    half = hidden_units // 2

    block = nodes // 4
    table = pl.pallas_call(
        table_kernel,
        grid=(nodes // block,),
        in_specs=[pl.BlockSpec((columns, block), lambda i: (0, i))],
        out_specs=pl.BlockSpec((block, 2, 128), lambda i: (i, 0, 0)),
        out_shape=jax.ShapeDtypeStruct((nodes, 2, 128), F32),
        compiler_params=pltpu.CompilerParams(vmem_limit_bytes=20 * MIB),
        cost_estimate=pl.CostEstimate(flops=0, bytes_accessed=24 * MIB, transcendentals=0),
        name="table",
    )(features)

    quarter = wide_count // 4 * 2 * capacity // 128
    blocks = [quarter] * 4 if capacity % 128 == 0 else [4 * quarter]
    parts = pl.pallas_call(
        functools.partial(list_kernel, wide_count, capacity, tgt_bits),
        out_shape=[jax.ShapeDtypeStruct((rows, 128), jnp.int32) for rows in blocks],
        compiler_params=pltpu.CompilerParams(vmem_limit_bytes=56 * MIB),
        name="lists",
    )(jnp.transpose(owner_of, (1, 2, 0)), jnp.transpose(row_of))
    if capacity % 128:
        both = jnp.transpose(parts[0].reshape(2, wide_count, capacity), (1, 0, 2))
        parts = list(both.reshape(4, wide_count // 4, 2 * capacity))
    bits = wide_count.bit_length() - 1
    weights = jnp.concatenate(
        [w_self, w_neighbor[128:], w_neighbor[:128]], axis=0
    )
    odd = swap(jnp.stack([parts[1], parts[3]]), "wide", 1)
    odd, table = lax.optimization_barrier((odd, table))
    high = swap(jnp.stack([parts[2], odd[1]]), "wide", 2)
    asked = jnp.stack([parts[0], odd[0], high[0], high[1]]).reshape(4, wide_count // 4, 2 * capacity)
    for b in range(2, bits):
        split = asked.reshape(asked.shape[0], -1, 2, 2 * capacity)
        asked = jnp.concatenate([split[:, :, 0], swap(split[:, :, 1], "wide", 1 << b)], axis=0)

    unroll = next(u for u in (128, 64, 32, 16, 8, 4, 2, 1) if capacity % u == 0)
    whole = pl.BlockSpec(memory_space=pltpu.VMEM)
    first = pl.pallas_call(
        functools.partial(first_kernel, unroll),
        grid_spec=pltpu.PrefetchScalarGridSpec(
            num_scalar_prefetch=1,
            grid=(1,),
            in_specs=[whole],
            out_specs=whole,
            scratch_shapes=[pltpu.VMEM((capacity, 2, 128), F32)],
        ),
        out_shape=jax.ShapeDtypeStruct((capacity, 256), BF16),
        compiler_params=pltpu.CompilerParams(vmem_limit_bytes=10 * MIB),
        cost_estimate=pl.CostEstimate(flops=0, bytes_accessed=4 * MIB, transcendentals=0),
        name="first",
    )(parts[0].reshape(-1), table)
    half_sums = (2, wide_count, share, 2 * columns)
    near_sums, beside_sums = pl.pallas_call(
        functools.partial(owner_kernel, tgt_bits),
        grid_spec=pltpu.PrefetchScalarGridSpec(
            num_scalar_prefetch=1,
            grid=(wide_count,),
            in_specs=[whole] * 3,
            out_specs=[
                pl.BlockSpec((2, 1, share, 2 * columns), lambda s, *_: (0, s, 0, 0))
            ] * 2,
            scratch_shapes=[
                pltpu.VMEM((capacity, 2, 128), F32),
                pltpu.VMEM((2, capacity, 256), BF16),
            ],
        ),
        out_shape=[jax.ShapeDtypeStruct(half_sums, BF16)] * 2,
        compiler_params=pltpu.CompilerParams(vmem_limit_bytes=30 * MIB),
        name="owner",
    )(asked.reshape(-1), asked.reshape(wide_count, 1, 2 * capacity), table, first)
    rows = 2 * wide_count * share
    ours = near_sums.reshape(rows, 2 * columns)
    theirs = beside_sums.reshape(rows, 2 * columns)
    far = ("narrow", (2,))
    steps = [("wide", (1 << b,)) for b in range(bits)]
    pair = ("wide", (2, 1))
    ways = [[far] + steps, [pair, far] + steps[2:]]
    backs = [steps[:1:-1] + [pair, far], steps[:1:-1] + [far, pair]]
    pieces = (2,) * (1 + bits) + (share, half)
    chains = []
    for c, way in enumerate(ways):
        columns_of = weights[:, c * half : (c + 1) * half]
        send = jnp.dot(theirs, columns_of, preferred_element_type=F32).astype(BF16)
        keep = lax.optimization_barrier(jnp.dot(ours, columns_of, preferred_element_type=F32))
        paired = keep.reshape(pieces) + swap(send, "narrow", 1).reshape(pieces)
        chains.append(jnp.transpose(paired, dims_of(way, bits) + [bits + 1, bits + 2]))
    for s in range(max(map(len, ways))):
        for c in (0, 1):
            if s < len(ways[c]):
                chains[c] = add_across(chains[c], *ways[c][s])
    preact = jnp.concatenate([chain.reshape(share, half) for chain in chains], axis=1)
    value, pullback = jax.vjp(activation, preact)
    hidden = value.astype(BF16)
    slope = pullback(cotangent.astype(F32))[0].astype(BF16)

    chains = [slope[:, :half], slope[:, half:]]
    for s in range(max(map(len, backs))):
        for c in (1, 0):
            if s < len(backs[c]):
                chains[c] = collect(chains[c], *backs[c][s])
    near = []
    for c, back in enumerate(backs):
        dims = dims_of(back[::-1], bits)
        order = [dims.index(d) for d in range(bits + 1)] + [bits + 1, bits + 2]
        whole_chain = chains[c].reshape((2,) * (1 + bits) + (share, half))
        near.append(jnp.transpose(whole_chain, order).reshape(-1, half))
    beside = [swap(n, "narrow", 1) for n in near]
    grads = contract_rows(ours, jnp.concatenate(near, axis=1)) + contract_rows(
        theirs, jnp.concatenate(beside, axis=1)
    )
    chains = [grads[:columns], grads[columns:]]
    turns = [steps, steps[1:] + steps[:1]]
    for s in range(len(turns[0])):
        for c in (0, 1):
            chains[c] = add_all(chains[c], *turns[c][s])
    grad_self, mixed = chains
    grad_neighbor = jnp.concatenate([mixed[columns - 128 :], mixed[: columns - 128]], axis=0)
    return (hidden, grad_self, grad_neighbor)


def solution(mesh):
    return jax.shard_map(
        on_device,
        mesh=mesh,
        in_specs=(
            P("narrow", "wide"),
            P("wide", None, None),
            P("wide", None),
            P("narrow", None),
            P("narrow", None),
            P(("wide", "narrow"), None),
        ),
        out_specs=(P(("wide", "narrow"), None), P("narrow", None), P("narrow", None)),
        check_vma=False,
    )
```
